128 devices in a mesh: expert: 32 (over y, z, core), shard: 4 (over x).
Axes of the slice: x: 4, y: 4, z: 4, core: 2. Of those that a mesh axis runs over, the one named last changes fastest.
Arguments:
- tokens: bfloat16 [32768, 2880], P('expert', 'shard'), may hold values from -6 to 6
- gate_weight: bfloat16 [64, 2880, 1536], P(None, 'expert', 'shard'), may hold values from -0.109375 to 0.109375
- up_weight: bfloat16 [64, 2880, 1536], P(None, 'expert', 'shard'), may hold values from -0.109375 to 0.109375
- down_weight: bfloat16 [64, 2880, 1536], P(None, 'expert', 'shard'), may hold values from -0.15625 to 0.15625
- block_counts: int32 [64], P('expert'), may hold values from 0 to 8, as said below
- block_tokens: int32 [256, 256], P('expert'), may hold values from 0 to 1023, as said below
Outputs:
- expert_out: bfloat16 [65536, 2880], P(('expert', 'shard'))
The draws below stay inside these ranges and needn't reach their ends.
Inputs may be any that keep to these rules, and one draw needn't show every extreme that they name: `block_counts`: for each section, the counts of its 2 experts sum to at most 8; some section is full in every draw. `block_tokens`: rows of the section's own dispatched tokens; every row of a section appears in exactly two positions of its slots.
All inputs are finite; a program needn't handle non-finite values.
Results may differ from the reference program's by a relative error of at most 0.015.
Values may be sent and summed in bfloat16 or wider, within the bound.
A program may use at most 256 MiB of HBM per device.

```python
import jax
import jax.numpy as jnp
from jax import lax

D = 2880
FFW = 1536
EXP_DEV = 2
GROUP = 32
BLOCK = 256
SLOTS = 8
EXPERTS = 64
ROWS_GRP = 1024
TOKENS = 32768
BLOCKS_ALL = 256
N_EXPERT = 32
N_SHARD = 4


def draw_block_counts(key, part):
    key = jax.random.fold_in(key, 11)
    first_key, second_key, third_key = jax.random.split(key, 3)
    sections = EXPERTS // EXP_DEV
    totals = jax.random.randint(first_key, (sections,), 1, SLOTS + 1)
    forced = jax.random.randint(second_key, (), 0, sections)
    place = jnp.arange(sections)
    totals = jnp.where(place == forced, SLOTS, totals)
    leading = jax.random.randint(third_key, (sections,), 0, 1 << 20) % (totals + 1)
    leading = jnp.where(place == forced, SLOTS, leading)
    counts = jnp.stack([leading, totals - leading], axis=-1)
    return counts.reshape(EXPERTS).astype(jnp.int32)


def draw_block_tokens(key, part):
    key = jax.random.fold_in(key, 23)
    sections = EXPERTS // EXP_DEV
    keys = jax.random.split(key, sections)

    def one_section(section_key):
        first = jax.random.permutation(jax.random.fold_in(section_key, 1), ROWS_GRP)
        second = jax.random.permutation(jax.random.fold_in(section_key, 2), ROWS_GRP)
        return jnp.concatenate([first, second]).astype(jnp.int32)
    table = jax.vmap(one_section)(keys)
    return table.reshape(sections * SLOTS, BLOCK).astype(jnp.int32)


def shard_levels(own_key, shape, cuts, low, high):
    def one(dim, blocks):
        draws = jax.random.uniform(jax.random.fold_in(jax.random.fold_in(own_key, 6), dim), (blocks,), jnp.float32, low / len(cuts), high / len(cuts))
        return jnp.repeat(jnp.exp(draws), shape[dim] // blocks).reshape((-1,) + (1,) * (len(shape) - dim - 1))

    level = one(*cuts[0])
    for cut in cuts[1:]:
        level = level * one(*cut)
    return level


def normal_values(own_key, dims, scale, reach, cuts=(), kind=jnp.bfloat16):
    loudness = shard_levels(own_key, dims, cuts, -0.22, 0.18) if cuts else 1.0
    values = jax.random.normal(own_key, dims, jnp.float32) * scale * loudness
    return jnp.minimum(jnp.maximum(values, -reach), reach).astype(kind)


def setup_inputs(seed: int = 0) -> dict:
    streams_of = jax.random.split(jax.random.key(seed), 7)
    return {
        "tokens": normal_values(streams_of[0], (TOKENS, D), 1.0, 6.0, ((0, 32), (1, 4))),
        "gate_weight": normal_values(streams_of[1], (EXPERTS, D, FFW), D ** -0.5, 0.109375, ((1, 32), (2, 4))),
        "up_weight": normal_values(streams_of[2], (EXPERTS, D, FFW), D ** -0.5, 0.109375, ((1, 32), (2, 4))),
        "down_weight": normal_values(streams_of[3], (EXPERTS, D, FFW), FFW ** -0.5, 0.15625, ((1, 32), (2, 4))),
        "block_counts": draw_block_counts(jax.random.fold_in(streams_of[6], 71), 0),
        "block_tokens": draw_block_tokens(jax.random.fold_in(streams_of[6], 71), 0),
    }


def shared_scale(amax):
    result = jnp.full(amax.shape, 2.0 ** -32, jnp.float32)
    for exponent in range(-29, 9):
        result = jnp.where(amax >= 2.0 ** exponent, jnp.float32(2.0 ** (exponent - 2)), result)
    return result


def nearest_code(ratio):
    magnitude = jnp.abs(ratio)
    level = 0.5 * (magnitude > 0.25).astype(jnp.float32)
    level = level + 0.5 * (magnitude >= 0.75).astype(jnp.float32)
    level = level + 0.5 * (magnitude > 1.25).astype(jnp.float32)
    level = level + 0.5 * (magnitude >= 1.75).astype(jnp.float32)
    level = level + (magnitude > 2.5).astype(jnp.float32)
    level = level + (magnitude >= 3.5).astype(jnp.float32)
    level = level + 2.0 * (magnitude > 5.0).astype(jnp.float32)
    return jnp.sign(ratio) * level


def restore_weights(weight):
    count, rows, cols = weight.shape
    grouped = weight.astype(jnp.float32).reshape(count, rows, cols // GROUP, GROUP)
    amax = jnp.max(jnp.abs(grouped), axis=-1)
    scales = shared_scale(amax).astype(jnp.bfloat16)
    coded = nearest_code(grouped / scales.astype(jnp.float32)[..., None]).astype(jnp.bfloat16)
    coded = lax.optimization_barrier(coded)
    restored = (coded.astype(jnp.float32) * scales.astype(jnp.float32)[..., None]).astype(jnp.bfloat16)
    return restored.reshape(count, rows, cols)


def activate(gate, up):
    return (up + 1.0) * gate * jax.nn.sigmoid(1.702 * gate)


def reference(tokens, gate_weight, up_weight, down_weight, block_counts, block_tokens):
    width = FFW // N_SHARD

    def section(group):
        group = group.astype(jnp.int32)
        rows = lax.dynamic_slice_in_dim(tokens, group * ROWS_GRP, ROWS_GRP, 0)
        counts = lax.dynamic_slice_in_dim(block_counts, group * EXP_DEV, EXP_DEV, 0)
        ids = lax.dynamic_slice_in_dim(block_tokens, group * SLOTS, SLOTS, 0)
        w_gate = restore_weights(lax.dynamic_slice_in_dim(gate_weight, group * EXP_DEV, EXP_DEV, 0))
        w_up = restore_weights(lax.dynamic_slice_in_dim(up_weight, group * EXP_DEV, EXP_DEV, 0))
        w_down = restore_weights(lax.dynamic_slice_in_dim(down_weight, group * EXP_DEV, EXP_DEV, 0))
        ends = jnp.cumsum(counts).astype(jnp.int32)

        def slot(index):
            index = index.astype(jnp.int32)
            local = jnp.sum((index >= ends[:-1]).astype(jnp.int32)).astype(jnp.int32)
            valid = index < ends[-1]

            def work(position):
                picked = jnp.take(rows, ids[position], axis=0)
                gate = jnp.dot(picked, w_gate[local], preferred_element_type=jnp.float32)
                up = jnp.dot(picked, w_up[local], preferred_element_type=jnp.float32)
                hidden = activate(gate, up).astype(jnp.bfloat16)
                split_hidden = hidden.astype(jnp.float32).reshape(BLOCK, N_SHARD, width)
                split_down = w_down[local].astype(jnp.float32).reshape(D, N_SHARD, width)
                partial_value = jnp.einsum("bsf,dsf->sbd", split_hidden, split_down).astype(jnp.bfloat16)
                return jnp.sum(partial_value.astype(jnp.float32), axis=0).astype(jnp.bfloat16)

            def skip(position):
                return jnp.zeros((BLOCK, D), jnp.bfloat16)

            return lax.cond(valid, work, skip, index)

        return lax.map(slot, jnp.arange(SLOTS, dtype=jnp.int32))

    result = lax.map(section, jnp.arange(N_EXPERT, dtype=jnp.int32))
    return result.reshape(BLOCKS_ALL * BLOCK, D)
```

```python
import functools

import jax
import jax.numpy as jnp
import numpy as np
from jax import lax
from jax.experimental import pallas as pl
from jax.experimental.pallas import tpu as pltpu
from jax.sharding import PartitionSpec as P

GROUP = 32
LANES = 128
BF16 = jnp.bfloat16
F32 = jnp.float32
MESH = pl.DeviceIdType.MESH

RING = 4
D = 2880
ROWS = 90
PAD = 96
FEAT = 720
WIDE = 8 * PAD
COLS = 384
TOK = 1024
BLOCK = 256
SLOTS = 8
TILE = 16
CHUNKS = 3
OUTB = 384


def place_matrix():
    m = np.zeros((FEAT, WIDE), np.float32)
    for k in range(FEAT):
        m[k, k // ROWS * PAD + k % ROWS] = 1
    return m


def group_matrix():
    lane = np.arange(LANES) // GROUP
    return (lane[:, None] == lane[None, :]).astype(np.float32)


def order_matrix():
    m = np.zeros((9, 12 * LANES, OUTB), np.float32)
    for d in range(D):
        pair, rest = divmod(d, 2 * ROWS)
        core, row = divmod(rest, ROWS)
        part, row = divmod(row, 48)
        chunk, row = divmod(row, TILE)
        half, pair = divmod(pair, 8)
        block, col = divmod(d, OUTB)
        if block == 3 and half == 1:
            block = 8
        m[block, ((2 * core + part) * CHUNKS + chunk) * LANES + pair * TILE + row, col] = 1
    return m


def power_floor(value):
    far = value * 8388609.0
    return far - (far - value)


def restore(weight, groups):
    power = power_floor(jnp.abs(weight) * 0.751953125)
    square = power * power
    sixth = (square * square) * (square * 2.0**60)
    total = jnp.dot(sixth.astype(BF16), groups, preferred_element_type=F32)
    top = power_floor(jnp.exp2((jnp.log2(total) - 60.0) * (1.0 / 6.0)) * 0.8)
    top = jnp.minimum(jnp.maximum(top, 2.0**-30), 2.0**8)
    magic = jnp.maximum(power, top * 0.25) * (1.5 * 2.0**22)
    rounded = (weight + magic) - magic
    limit = top * 1.5
    return jnp.minimum(jnp.maximum(rounded, -limit), limit).astype(BF16)


def kernel(
    tokens, gate_w, up_w, down_w, sel, expert, place, groups, order,
    out, mid, xs, midd,
    ob, inbox, tok, stage, in_0, in_1, in_2, hid2, hid, ob_out, fin,
    stage_sem, order_sem, s1_send, s1_recv, s2_send, s2_recv, xs_send, xs_recv,
    d1_send, d1_recv, d2_send, d2_recv, tok_send, tok_recv, hid_send, hid_recv, out_send, out_recv,
):
    in_d = (in_0, in_1, in_2)
    me, x = lax.axis_index("expert"), lax.axis_index("shard")
    y, z, c = me // 8, (me // 2) % 4, me % 2

    def device(yy, zz, cc, xx):
        return ((yy * 4 + zz) * 2 + cc, xx)

    def ring(at, step):
        return (at + step) % RING

    def remote(src, dst, send, recv, target):
        return pltpu.make_async_remote_copy(
            src_ref=src, dst_ref=dst, send_sem=send, recv_sem=recv, device_id=target, device_id_type=MESH
        )

    def landed(ref, sem):
        pltpu.make_async_copy(ref, ref, sem).wait()

    barrier = pltpu.get_barrier_semaphore()
    peers = [device(y, z, 1 - c, x)]
    for step in (1, 2, 3):
        for cc in (c, 1 - c):
            peers += [device(ring(y, step), z, cc, x), device(y, ring(z, step), cc, x), device(y, z, cc, ring(x, step))]
    for peer in peers:
        pl.semaphore_signal(barrier, inc=1, device_id=peer, device_id_type=MESH)

    def load(n, slot):
        q, step = n // 4, (n + 1) % 4
        return [
            pltpu.make_async_copy(gate_w.at[ring(y, step), :, :, q], stage.at[slot, 0], stage_sem.at[slot, 0]),
            pltpu.make_async_copy(up_w.at[:, ring(z, step), :, q], stage.at[slot, 1], stage_sem.at[slot, 1]),
        ]

    def load_down(n, slot):
        return [
            pltpu.make_async_copy(down_w.at[n, :, :, e], stage.at[slot, e], stage_sem.at[slot, e]) for e in (0, 1)
        ]

    for copy in load(0, 0):
        copy.start()

    @pl.loop(0, 128)
    def _(n):
        ob[n // 64, n % 64, 80:PAD, :] = jnp.zeros((16, COLS), BF16)

    @pl.loop(0, 4)
    def _(n):
        rows = pl.ds(n * 256, 256)
        tok[x, rows, :] = jnp.dot(tokens[rows, :], place[...], preferred_element_type=F32).astype(BF16)

    pl.semaphore_wait(barrier, len(peers))

    right, left = device(y, z, c, ring(x, 1)), device(y, z, c, ring(x, 3))
    tok_near = [
        remote(tok.at[x], tok.at[x], tok_send.at[0], tok_recv.at[0], right),
        remote(tok.at[x], tok.at[x], tok_send.at[1], tok_recv.at[1], left),
    ]
    for copy in tok_near:
        copy.start()
    lower, upper = pl.ds(0, 512), pl.ds(512, 512)
    tok_far = [
        remote(tok.at[ring(x, 3), lower], tok.at[ring(x, 3), lower], tok_send.at[2], tok_recv.at[2], right),
        remote(tok.at[ring(x, 1), upper], tok.at[ring(x, 1), upper], tok_send.at[3], tok_recv.at[3], left),
    ]

    def encode(slot, i, dst):
        half, zc = i // 8, i % 8
        for lane in range(COLS // LANES):
            cols = slice(lane * LANES, (lane + 1) * LANES)
            weight = stage[slot, half, zc // 2, zc % 2, :, cols].astype(F32)
            ob[dst[0], dst[1], 0:ROWS, cols] = restore(weight, groups[...])

    def first(ab, q, step):
        to = ring(y, step) if ab == 0 else ring(z, step)
        target = device(to, z, c, x) if ab == 0 else device(y, to, c, x)
        here = y if ab == 0 else z
        src, dst = ob.at[q, pl.ds(32 * ab + to * 8, 8)], mid.at[ab, q, here]
        return src, dst, s1_send.at[ab, q, step], s1_recv.at[ab, q, step], target

    @pl.loop(0, 8)
    def _(n):
        slot, q, step = n % 2, n // 4, (n + 1) % 4
        for copy in load(n, slot):
            copy.wait()

        @pl.when(n < 7)
        def _():
            for copy in load(n + 1, 1 - slot):
                copy.start()

        @pl.loop(0, 16, unroll=4)
        def _(i):
            half = i // 8
            to = (1 - half) * ring(y, step) + half * (4 + ring(z, step))
            encode(slot, i, (q, to * 8 + i % 8))

        @pl.when(step == 0)
        def _():
            for ab in (0, 1):
                src, dst, _, recv, _ = first(ab, q, 0)
                pltpu.make_async_copy(src, dst, recv).start()

        @pl.when(step != 0)
        def _():
            for ab in (0, 1):
                remote(*first(ab, q, step)).start()

    for copy in load_down(0, 0):
        copy.start()

    def second(q):
        local, far = [], []
        for step in (2, 1, 3, 0):
            for dc in (0, 1):
                cc = (c + dc) % 2
                zz, yy = ring(z, step), ring(y, step)
                a = (mid.at[0, q, :, zz * 2 + cc], inbox.at[pl.ds(q * 8, 4), z, c])
                b = (mid.at[1, q, :, yy * 2 + cc], inbox.at[q * 8 + 4 + y, :, c])
                if step == 0 and dc == 0:
                    local += [pltpu.make_async_copy(*pair, s2_recv.at[ab, q, 0, 0]) for ab, pair in enumerate((a, b))]
                    continue
                for ab, pair, target in ((0, a, device(y, zz, cc, x)), (1, b, device(yy, z, cc, x))):
                    far.append(remote(*pair, s2_send.at[ab, q, step, dc], s2_recv.at[ab, q, step, dc], target))
        return local, far

    def pass_on(q):
        for ab in (0, 1):
            for step in range(RING):
                _, dst, _, recv, _ = first(ab, q, step)
                landed(dst, recv)
        local, far = second(q)
        for copy in far + local:
            copy.start()
        return local, far

    def sent(q):
        for ab in (0, 1):
            for step in (1, 2, 3):
                remote(*first(ab, q, step)).wait_send()

    second_0 = pass_on(0)
    for near, far in zip(tok_near, tok_far):
        near.wait_recv()
        far.start()

    sent(0)

    @pl.loop(0, 4)
    def _(n):
        slot = n % 2
        for copy in load_down(n, slot):
            copy.wait()

        @pl.when(n < 3)
        def _():
            for copy in load_down(n + 1, 1 - slot):
                copy.start()

        @pl.loop(0, 16, unroll=4)
        def _(i):
            e, zz, cc = i // 8, (i // 2) % 4, i % 2
            encode(slot, i, (0, cc * 32 + (1 - e) * (n * 4 + zz) + e * (16 + zz * 4 + n)))

    shuffles = []
    for cc in (0, 1):
        for h in (0, 1):
            to = 2 * c + h
            src, dst = ob.at[0, pl.ds(cc * 32, 32), pl.ds(48 * h, 48)], xs.at[x]
            own = jnp.logical_and(cc == c, to == x)
            far = remote(src, dst, xs_send.at[cc, h], xs_recv.at[x], device(y, z, cc, to))
            near = pltpu.make_async_copy(src, dst, xs_recv.at[x])
            pl.when(own)(near.start)
            pl.when(jnp.logical_not(own))(far.start)
            shuffles.append((own, far))

    second_1 = pass_on(1)

    def arrived(copies):
        local, far = copies
        for copy in local:
            copy.wait()
        for copy in far:
            copy.wait_recv()

    def hidden(q):
        @pl.loop(0, 4)
        def _(n):
            rows = pl.ds(n * 256, 256)
            gate = up = None
            for s in range(RING):
                picked = tok[s, rows, :]
                w_gate = inbox[q * 8 + s].reshape(WIDE, COLS)
                w_up = inbox[q * 8 + 4 + s].reshape(WIDE, COLS)
                g = jnp.dot(picked, w_gate, preferred_element_type=F32)
                u = jnp.dot(picked, w_up, preferred_element_type=F32)
                gate, up = (g, u) if gate is None else (gate + g, up + u)
            hid2[q, rows, :] = ((up + 1.0) * gate * jax.nn.sigmoid(1.702 * gate)).astype(BF16)

    arrived(second_0)
    for copy in tok_far:
        copy.wait_recv()
    hidden(0)

    for n in range(RING):
        landed(xs.at[n], xs_recv.at[n])

    def down_first(r):
        local, far = [], []
        for step in (2, 1, 3, 0):
            yy, zz = ring(y, step), ring(z, step)
            rows = pl.ds(r * TILE, TILE)
            a = (xs.at[:, pl.ds(yy * 4, 4), rows], midd.at[0, r, :, y])
            b = (xs.at[:, pl.ds(16 + zz * 4, 4), rows], midd.at[1, r, :, z])
            if step == 0:
                local += [pltpu.make_async_copy(*pair, d1_recv.at[ab, r, 0]) for ab, pair in enumerate((a, b))]
                continue
            for ab, pair, target in ((0, a, device(yy, z, c, x)), (1, b, device(y, zz, c, x))):
                far.append(remote(*pair, d1_send.at[ab, r, step], d1_recv.at[ab, r, step], target))
        return local, far

    def down_second(r):
        local, far = [], []
        for step in (2, 1, 3, 0):
            yy, zz = ring(y, step), ring(z, step)
            a = (midd.at[0, r, :, :, zz], in_d[r].at[0, :, :, z])
            b = (midd.at[1, r, :, :, yy], in_d[r].at[1, :, y])
            if step == 0:
                local += [pltpu.make_async_copy(*pair, d2_recv.at[ab, r, 0]) for ab, pair in enumerate((a, b))]
                continue
            for ab, pair, target in ((0, a, device(y, zz, c, x)), (1, b, device(yy, z, c, x))):
                far.append(remote(*pair, d2_send.at[ab, r, step], d2_recv.at[ab, r, step], target))
        return local, far

    def start(copies):
        for copy in copies[1] + copies[0]:
            copy.start()

    down_1 = [down_first(r) for r in range(CHUNKS)]
    down_2 = [down_second(r) for r in range(CHUNKS)]
    for copies in down_1:
        start(copies)

    arrived(second_1)
    hidden(1)

    load_order = pltpu.make_async_copy(order, inbox, order_sem)
    load_order.start()

    lanes = lax.broadcasted_iota(jnp.int32, (BLOCK, TOK), 1)
    hid_near, hid_far = [], []
    for h in (0, 1):
        @pl.loop(0, 4)
        def _(n):
            slot = 2 * n + h
            pick = (sel[slot] == lanes).astype(F32).astype(BF16)
            hid[x, h, n] = jnp.dot(pick, hid2[expert[slot]], preferred_element_type=F32).astype(BF16)

        own, below, above = hid.at[x, h], hid.at[ring(x, 3), h, pl.ds(0, 2)], hid.at[ring(x, 1), h, pl.ds(2, 2)]
        hid_near.append([
            remote(own, own, hid_send.at[h, 0], hid_recv.at[h, 0], right),
            remote(own, own, hid_send.at[h, 1], hid_recv.at[h, 1], left),
        ])
        hid_far.append([
            remote(below, below, hid_send.at[h, 2], hid_recv.at[h, 2], right),
            remote(above, above, hid_send.at[h, 3], hid_recv.at[h, 3], left),
        ])
        for copy in hid_near[h]:
            copy.start()

    def hid_forward(h):
        for near, far in zip(hid_near[h], hid_far[h]):
            near.wait_recv()
            far.start()

    arrived(down_1[0])
    start(down_2[0])
    hid_forward(0)
    arrived(down_1[1])
    start(down_2[1])
    hid_forward(1)
    arrived(down_1[2])
    start(down_2[2])

    results = []

    def project(h, r):
        for step in (2, 1, 3, 0):
            to = ring(x, step)
            which = expert[2 * to + h]
            total = None
            for s in range(RING):
                part = lax.dot_general(
                    hid[s, h, to],
                    in_d[r][which, s].reshape(BLOCK, COLS),
                    (((1,), (1,)), ((), ())),
                    preferred_element_type=F32,
                )
                total = part if total is None else total + part
            if step == 0:
                fin[x, h, r] = total.astype(BF16)
                continue
            ob_out[step - 1, h, r] = total.astype(BF16)
            copy = remote(
                ob_out.at[step - 1, h, r], fin.at[x, h, r], out_send.at[h, r, step - 1], out_recv.at[h, r, step - 1],
                device(y, z, c, to),
            )
            copy.start()
            results.append((h, r, copy))

    for copy in hid_far[0]:
        copy.wait_recv()
    arrived(down_2[0])
    project(0, 0)
    arrived(down_2[1])
    project(0, 1)
    for copy in hid_far[1]:
        copy.wait_recv()
    project(1, 0)
    project(1, 1)
    arrived(down_2[2])
    project(0, 2)
    project(1, 2)

    load_order.wait()

    def ordered(h, half, matrix):
        lhs = jnp.concatenate(
            [fin[s, h, r, :, half * LANES : (half + 1) * LANES] for s in range(RING) for r in range(CHUNKS)], axis=1
        )
        return jnp.dot(lhs, inbox[pl.ds(2 * matrix, 2)].reshape(12 * LANES, OUTB), preferred_element_type=F32)

    for h in (0, 1):
        for hh, _, copy in results:
            if hh == h:
                copy.wait_recv()
        rows = slice(h * BLOCK, (h + 1) * BLOCK)

        @pl.loop(0, 3)
        def _(b):
            out[rows, pl.ds(pl.multiple_of(b * OUTB, OUTB), OUTB)] = ordered(h, 0, b).astype(BF16)

        out[rows, 3 * OUTB : 4 * OUTB] = (ordered(h, 0, 3) + ordered(h, 1, 8)).astype(BF16)

        @pl.loop(4, 7)
        def _(b):
            out[rows, pl.ds(pl.multiple_of(b * OUTB, OUTB), OUTB)] = ordered(h, 1, b).astype(BF16)

        out[rows, 7 * OUTB : D] = ordered(h, 1, 7)[:, : D - 7 * OUTB].astype(BF16)

    sent(1)
    for own, far in shuffles:
        pl.when(jnp.logical_not(own))(far.wait_send)
    for copies in (second_0, second_1, *down_1, *down_2):
        for copy in copies[1]:
            copy.wait_send()
    for copy in tok_near + tok_far + sum(hid_near + hid_far, []) + [copy for _, _, copy in results]:
        copy.wait_send()


def body(tokens, gate_weight, up_weight, down_weight, block_counts, block_tokens):
    total = jnp.sum(block_counts)
    slot = jnp.arange(SLOTS, dtype=jnp.int32)
    expert = (slot >= block_counts[0]).astype(jnp.int32)
    sel = jnp.where((slot < total)[:, None], block_tokens, -1)[:, :, None]
    split = (RING, RING, 2, 2, ROWS, COLS)
    vmem, hbm = pl.BlockSpec(memory_space=pltpu.VMEM), pl.BlockSpec(memory_space=pltpu.HBM)
    dma = pltpu.SemaphoreType.DMA
    made = pl.pallas_call(
        kernel,
        out_shape=(
            jax.ShapeDtypeStruct((2 * BLOCK, D), BF16),
            jax.ShapeDtypeStruct((2, 2, RING, 8, PAD, COLS), BF16),
            jax.ShapeDtypeStruct((RING, 32, 48, COLS), BF16),
            jax.ShapeDtypeStruct((2, CHUNKS, RING, RING, RING, TILE, COLS), BF16),
        ),
        in_specs=[vmem, hbm, hbm, hbm, vmem, pl.BlockSpec(memory_space=pltpu.SMEM), vmem, vmem, hbm],
        out_specs=(vmem, hbm, hbm, hbm),
        scratch_shapes=[
            pltpu.VMEM((2, 64, PAD, COLS), BF16),
            pltpu.VMEM((18, RING, 2, PAD, COLS), BF16),
            pltpu.VMEM((RING, TOK, WIDE), BF16),
            pltpu.VMEM((2, 2, RING, 2, ROWS, COLS), BF16),
            *[pltpu.VMEM((2, RING, RING, RING, TILE, COLS), BF16) for _ in range(CHUNKS)],
            pltpu.VMEM((2, TOK, COLS), BF16),
            pltpu.VMEM((RING, 2, RING, BLOCK, COLS), BF16),
            pltpu.VMEM((3, 2, CHUNKS, BLOCK, BLOCK), BF16),
            pltpu.VMEM((RING, 2, CHUNKS, BLOCK, BLOCK), BF16),
            dma((2, 2)),
            dma,
            dma((2, 2, RING)), dma((2, 2, RING)),
            dma((2, 2, RING, 2)), dma((2, 2, RING, 2)),
            dma((2, 2)), dma((RING,)),
            dma((2, CHUNKS, RING)), dma((2, CHUNKS, RING)),
            dma((2, CHUNKS, RING)), dma((2, CHUNKS, RING)),
            dma((RING,)), dma((RING,)),
            dma((2, RING)), dma((2, RING)),
            dma((2, CHUNKS, 3)), dma((2, CHUNKS, 3)),
        ],
        compiler_params=pltpu.CompilerParams(
            collective_id=0, has_side_effects=True, vmem_limit_bytes=60 * 2**20
        ),
    )(
        tokens,
        gate_weight.reshape(split),
        up_weight.reshape(split),
        down_weight.reshape(split),
        sel,
        expert,
        jnp.asarray(place_matrix(), BF16),
        jnp.asarray(group_matrix(), BF16),
        jnp.asarray(order_matrix(), BF16).reshape(18, RING, 2, PAD, COLS),
    )
    return made[0]


def solution(mesh):
    in_specs = (
        P("expert", "shard"),
        P(None, "expert", "shard"),
        P(None, "expert", "shard"),
        P(None, "expert", "shard"),
        P("expert"),
        P("expert", None),
    )
    out_specs = P(("expert", "shard"), None)
    return jax.shard_map(body, mesh=mesh, in_specs=in_specs, out_specs=out_specs, check_vma=False)
```

```python
import functools

import jax
import jax.numpy as jnp
import numpy as np
from jax import lax
from jax.experimental import pallas as pl
from jax.experimental.pallas import tpu as pltpu
from jax.sharding import PartitionSpec as P

GROUP = 32
LANES = 128
BF16 = jnp.bfloat16
F32 = jnp.float32
MESH = pl.DeviceIdType.MESH

RING = 4
D = 2880
ROWS = 90
PAD = 96
FEAT = 720
WIDE = 8 * PAD
COLS = 384
TOK = 1024
BLOCK = 256
SLOTS = 8
TILE = 16
CHUNKS = 3
OUTB = 384


def place_matrix():
    m = np.zeros((FEAT, WIDE), np.float32)
    for k in range(FEAT):
        j, row = divmod(k, ROWS)
        m[k, row // 48 * (WIDE // 2) + j * 48 + row % 48] = 1
    return m


def group_matrix():
    lane = np.arange(LANES) // GROUP
    return (lane[:, None] == lane[None, :]).astype(np.float32)


def swap_matrix():
    m = np.zeros((BLOCK, BLOCK), np.float32)
    for k in range(BLOCK):
        m[k, k % 16 * 16 + k // 16] = 1
    return m


def order_matrix():
    m = np.zeros((9, RING, OUTB, OUTB), np.float32)
    for d in range(D):
        pair, rest = divmod(d, 2 * ROWS)
        core, row = divmod(rest, ROWS)
        part, row = divmod(row, 48)
        chunk, row = divmod(row, TILE)
        half, pair = divmod(pair, 8)
        block, col = divmod(d, OUTB)
        if block == 3 and half == 1:
            block = 8
        m[block, 2 * core + part, col, chunk * LANES + pair * TILE + row] = 1
    return m


def power_floor(value):
    far = value * 8388609.0
    return far - (far - value)


def restore(weight, groups):
    power = power_floor(jnp.abs(weight) * 0.751953125)
    square = power * power
    sixth = (square * square) * (square * 2.0**60)
    total = jnp.dot(sixth.astype(BF16), groups, preferred_element_type=F32)
    top = power_floor(jnp.exp2((jnp.log2(total) - 60.0) * (1.0 / 6.0)) * 0.8)
    top = jnp.minimum(jnp.maximum(top, 2.0**-30), 2.0**8)
    magic = jnp.maximum(power, top * 0.25) * (1.5 * 2.0**22)
    rounded = (weight + magic) - magic
    limit = top * 1.5
    return jnp.minimum(jnp.maximum(rounded, -limit), limit).astype(BF16)


def kernel(
    tokens, gate_w, up_w, down_w, block_tokens, counts, place, groups, swap, order,
    out, mid, xs, midd,
    ob, inbox, tok, stage, in_0, in_1, in_2, hid2, hid, ob_out, fin, picks, sums,
    stage_sem, order_sem, s1_send, s1_recv, s2_send, s2_recv, xs_send, xs_recv,
    d1_send, d1_recv, d2_send, d2_recv, tok_send, tok_recv, hid_send, hid_recv, out_send, out_recv,
):
    in_d = (in_0, in_1, in_2)
    me, x = lax.axis_index("expert"), lax.axis_index("shard")
    y, z, c = me // 8, (me // 2) % 4, me % 2

    def device(yy, zz, cc, xx):
        return ((yy * 4 + zz) * 2 + cc, xx)

    def ring(at, step):
        return (at + step) % RING

    def remote(src, dst, send, recv, target):
        return pltpu.make_async_remote_copy(
            src_ref=src, dst_ref=dst, send_sem=send, recv_sem=recv, device_id=target, device_id_type=MESH
        )

    def landed(ref, sem):
        pltpu.make_async_copy(ref, ref, sem).wait()

    barrier = pltpu.get_barrier_semaphore()
    peers = [device(y, z, 1 - c, x)]
    for step in (1, 2, 3):
        for cc in (c, 1 - c):
            peers += [device(ring(y, step), z, cc, x), device(y, ring(z, step), cc, x), device(y, z, cc, ring(x, step))]
    for peer in peers:
        pl.semaphore_signal(barrier, inc=1, device_id=peer, device_id_type=MESH)

    def load(weight, q, yy, slot, ab):
        experts = pl.ds(yy * 16, 16)
        main = pltpu.make_async_copy(
            weight.at[pl.ds(q * 48, 42), experts], stage.at[slot, ab, 0:42], stage_sem.at[slot, ab, 0]
        )
        rest = pltpu.make_async_copy(weight.at[42:48, experts], stage.at[slot, ab, 42:48], stage_sem.at[slot, ab, 1])
        return main, rest

    def load_start(weight, q, yy, slot, ab):
        main, rest = load(weight, q, yy, slot, ab)
        main.start()
        pl.when(q == 0)(rest.start)

    def load_wait(weight, q, yy, slot, ab):
        main, rest = load(weight, q, yy, slot, ab)
        main.wait()
        pl.when(q == 0)(rest.wait)

        @pl.when(q == 1)
        def _():
            stage[slot, ab, 42:48] = jnp.zeros((6, 16, COLS), BF16)

    load_start(gate_w, 0, ring(y, 1), 0, 0)
    load_start(up_w, 0, 0, 0, 1)
    picks[...] = jnp.transpose(block_tokens[...])

    @pl.loop(0, 4)
    def _(n):
        rows = pl.ds(pl.multiple_of(n * 256, 256), 256)
        tok[x, rows, :] = lax.dot_general(
            tokens[:, rows], place[...], (((0,), (0,)), ((), ())), preferred_element_type=F32
        ).astype(BF16)

    pl.semaphore_wait(barrier, len(peers))

    right, left = device(y, z, c, ring(x, 1)), device(y, z, c, ring(x, 3))
    tok_near = [
        remote(tok.at[x], tok.at[x], tok_send.at[0], tok_recv.at[0], right),
        remote(tok.at[x], tok.at[x], tok_send.at[1], tok_recv.at[1], left),
    ]
    for copy in tok_near:
        copy.start()
    lower, upper = pl.ds(0, 512), pl.ds(512, 512)
    tok_far = [
        remote(tok.at[ring(x, 3), lower], tok.at[ring(x, 3), lower], tok_send.at[2], tok_recv.at[2], right),
        remote(tok.at[ring(x, 1), upper], tok.at[ring(x, 1), upper], tok_send.at[3], tok_recv.at[3], left),
    ]

    def encode(slot, ab, to):
        @pl.loop(0, 3, unroll=3)
        def _(j):
            rows = pl.ds(pl.multiple_of(j * TILE, TILE), TILE)
            for lane in range(COLS // LANES):
                cols = slice(lane * LANES, (lane + 1) * LANES)
                block = stage[slot, ab, rows, :, cols].reshape(BLOCK, LANES)
                for zz in range(RING):
                    weight = jnp.dot(swap[zz * 64 : zz * 64 + 64, :], block, preferred_element_type=F32)
                    ob[*to, zz, :, :, rows, cols] = restore(weight, groups[...]).reshape(2, 2, TILE, LANES)

    def first_y(q, step):
        to = ring(y, step)
        return ob.at[0, q, to], mid.at[0, q, y], s1_send.at[0, q, step], s1_recv.at[0, q, step], device(to, z, c, x)

    def first_z(q, step, yy):
        to = ring(z, step)
        send, recv = s1_send.at[1, q, step], s1_recv.at[1, q, step]
        return ob.at[1, q, yy, to], mid.at[1, q, z, yy], send, recv, device(y, to, c, x)

    @pl.loop(0, 8)
    def _(n):
        slot, q, i = n % 2, n // 4, n % 4
        load_wait(gate_w, q, ring(y, i + 1), slot, 0)
        load_wait(up_w, q, i, slot, 1)

        @pl.when(n < 7)
        def _():
            load_start(gate_w, (n + 1) // 4, ring(y, n + 2), 1 - slot, 0)
            load_start(up_w, (n + 1) // 4, (n + 1) % 4, 1 - slot, 1)

        encode(slot, 0, (0, q, ring(y, i + 1)))

        @pl.when(i == 3)
        def _():
            src, dst, _, recv, _ = first_y(q, 0)
            pltpu.make_async_copy(src, dst, recv).start()

        @pl.when(i != 3)
        def _():
            remote(*first_y(q, i + 1)).start()

        encode(slot, 1, (1, q, i))
        for step in (2, 1, 3):
            remote(*first_z(q, step, i)).start()
        src, dst, _, recv, _ = first_z(q, 0, i)
        pltpu.make_async_copy(src, dst, recv).start()

    load_start(down_w, 0, 0, 0, 0)
    everything = slice(None)

    def second(q):
        local, far = [], []
        rows = pl.ds(q * 48, 48)
        for step in (2, 1, 3, 0):
            for dc in (0, 1):
                cc = (c + dc) % 2
                zz, yy = ring(z, step), ring(y, step)
                a = (mid.at[0, q, :, zz, cc], inbox.at[0:4, z, c, :, rows])
                b = (mid.at[1, q, :, yy, cc], inbox.at[4 + y, :, c, :, rows])
                if step == 0 and dc == 0:
                    local += [pltpu.make_async_copy(*pair, s2_recv.at[ab, q, 0, 0]) for ab, pair in enumerate((a, b))]
                    continue
                for ab, pair, target in ((0, a, device(y, zz, cc, x)), (1, b, device(yy, z, cc, x))):
                    far.append(remote(*pair, s2_send.at[ab, q, step, dc], s2_recv.at[ab, q, step, dc], target))
        return local, far

    def pass_on(q):
        for step in range(RING):
            landed(mid.at[0, q, y], s1_recv.at[0, q, step])
            landed(mid.at[1, q, z], s1_recv.at[1, q, step])
        local, far = second(q)
        for copy in far + local:
            copy.start()
        return local, far

    def sent(q):
        for step in (1, 2, 3):
            remote(*first_y(q, step)).wait_send()
            remote(*first_z(q, step, everything)).wait_send()

    second_0 = pass_on(0)
    for near, far in zip(tok_near, tok_far):
        near.wait_recv()
        far.start()

    sent(0)

    @pl.loop(0, 8)
    def _(n):
        slot, h, yy = n % 2, n // 4, n % 4
        load_wait(down_w, h, yy, slot, 0)

        @pl.when(n < 7)
        def _():
            load_start(down_w, (n + 1) // 4, (n + 1) % 4, 1 - slot, 0)

        encode(slot, 0, (h, 0, yy))

    shuffles = []
    for cc in (0, 1):
        for h in (0, 1):
            to = 2 * c + h
            src, dst = ob.at[h, 0, :, :, cc], xs.at[x]
            own = jnp.logical_and(cc == c, to == x)
            far = remote(src, dst, xs_send.at[cc, h], xs_recv.at[x], device(y, z, cc, to))
            near = pltpu.make_async_copy(src, dst, xs_recv.at[x])
            pl.when(own)(near.start)
            pl.when(jnp.logical_not(own))(far.start)
            shuffles.append((own, far))

    second_1 = pass_on(1)

    def arrived(copies):
        local, far = copies
        for copy in local:
            copy.wait()
        for copy in far:
            copy.wait_recv()

    def products(q):
        @pl.loop(0, 8)
        def _(n):
            e, rows = n // 4, pl.ds(pl.multiple_of(n % 4 * 256, 256), 256)
            made = []
            for ab in (0, 1):
                total = None if q == 0 else sums[e, ab, rows, :]
                for s in range(RING):
                    weight = inbox[4 * ab + s, :, :, e, q * 48 : q * 48 + 48].reshape(WIDE // 2, COLS)
                    picked = tok[s, rows, q * (WIDE // 2) : (q + 1) * (WIDE // 2)]
                    part = jnp.dot(picked, weight, preferred_element_type=F32)
                    total = part if total is None else total + part
                made.append(total)
            if q == 0:
                sums[e, 0, rows, :], sums[e, 1, rows, :] = made
            else:
                gate, up = made
                hid2[e, rows, :] = ((up + 1.0) * gate * jax.nn.sigmoid(1.702 * gate)).astype(BF16)

    arrived(second_0)
    for copy in tok_far:
        copy.wait_recv()
    products(0)

    for n in range(RING):
        landed(xs.at[n], xs_recv.at[n])

    def down_first(r):
        local, far = [], []
        for step in (2, 1, 3, 0):
            yy, zz = ring(y, step), ring(z, step)
            rows = pl.ds(r * TILE, TILE)
            a = (xs.at[:, yy, :, 0, rows], midd.at[0, r, :, y])
            b = (xs.at[:, :, zz, 1, rows], midd.at[1, r, :, z])
            if step == 0:
                local += [pltpu.make_async_copy(*pair, d1_recv.at[ab, r, 0]) for ab, pair in enumerate((a, b))]
                continue
            for ab, pair, target in ((0, a, device(yy, z, c, x)), (1, b, device(y, zz, c, x))):
                far.append(remote(*pair, d1_send.at[ab, r, step], d1_recv.at[ab, r, step], target))
        return local, far

    def down_second(r):
        local, far = [], []
        for step in (2, 1, 3, 0):
            yy, zz = ring(y, step), ring(z, step)
            a = (midd.at[0, r, :, :, zz], in_d[r].at[0, :, :, z])
            b = (midd.at[1, r, :, :, yy], in_d[r].at[1, :, y])
            if step == 0:
                local += [pltpu.make_async_copy(*pair, d2_recv.at[ab, r, 0]) for ab, pair in enumerate((a, b))]
                continue
            for ab, pair, target in ((0, a, device(y, zz, c, x)), (1, b, device(yy, z, c, x))):
                far.append(remote(*pair, d2_send.at[ab, r, step], d2_recv.at[ab, r, step], target))
        return local, far

    def start(copies):
        for copy in copies[1] + copies[0]:
            copy.start()

    down_1 = [down_first(r) for r in range(CHUNKS)]
    down_2 = [down_second(r) for r in range(CHUNKS)]
    for copies in down_1:
        start(copies)

    arrived(second_1)
    products(1)

    load_order = pltpu.make_async_copy(order, inbox, order_sem)
    load_order.start()

    first, total = counts[0], counts[0] + counts[1]
    lanes = lax.broadcasted_iota(jnp.int32, (BLOCK, TOK), 1)
    hid_near, hid_far = [], []
    for h in (0, 1):
        for n in range(RING):
            slot = 2 * n + h
            row = jnp.where(slot < total, picks[:, slot : slot + 1], -1)
            pick = (row == lanes).astype(F32).astype(BF16)
            which = (slot >= first).astype(jnp.int32)
            hid[x, h, n] = jnp.dot(pick, hid2[which], preferred_element_type=F32).astype(BF16)

        own, below, above = hid.at[x, h], hid.at[ring(x, 3), h, pl.ds(0, 2)], hid.at[ring(x, 1), h, pl.ds(2, 2)]
        hid_near.append([
            remote(own, own, hid_send.at[h, 0], hid_recv.at[h, 0], right),
            remote(own, own, hid_send.at[h, 1], hid_recv.at[h, 1], left),
        ])
        hid_far.append([
            remote(below, below, hid_send.at[h, 2], hid_recv.at[h, 2], right),
            remote(above, above, hid_send.at[h, 3], hid_recv.at[h, 3], left),
        ])
        for copy in hid_near[h]:
            copy.start()

    def hid_forward(h):
        for near, far in zip(hid_near[h], hid_far[h]):
            near.wait_recv()
            far.start()

    arrived(down_1[0])
    start(down_2[0])
    hid_forward(0)
    arrived(down_1[1])
    start(down_2[1])
    hid_forward(1)
    arrived(down_1[2])
    start(down_2[2])

    results = []

    def project(h, r):
        for step in (2, 1, 3, 0):
            to = ring(x, step)
            which = (2 * to + h >= first).astype(jnp.int32)
            made = None
            for s in range(RING):
                part = lax.dot_general(
                    hid[s, h, to],
                    in_d[r][which, s].reshape(BLOCK, COLS),
                    (((1,), (1,)), ((), ())),
                    preferred_element_type=F32,
                )
                made = part if made is None else made + part
            if step == 0:
                fin[x, h, r] = made.astype(BF16)
                continue
            ob_out[step - 1, h, r] = made.astype(BF16)
            copy = remote(
                ob_out.at[step - 1, h, r], fin.at[x, h, r], out_send.at[h, r, step - 1], out_recv.at[h, r, step - 1],
                device(y, z, c, to),
            )
            copy.start()
            results.append((h, r, copy))

    for copy in hid_far[0]:
        copy.wait_recv()
    arrived(down_2[0])
    project(0, 0)
    arrived(down_2[1])
    project(0, 1)
    for copy in hid_far[1]:
        copy.wait_recv()
    project(1, 0)
    project(1, 1)
    arrived(down_2[2])
    project(0, 2)
    project(1, 2)

    load_order.wait()

    def ordered(h, half, matrix):
        result = None
        table = inbox[matrix].reshape(RING * OUTB, OUTB)
        for n in range(RING):
            got = [fin[n, h, r, :, half * LANES : (half + 1) * LANES] for r in range(CHUNKS)]
            part = lax.dot_general(
                table[n * OUTB : (n + 1) * OUTB],
                jnp.concatenate(got, axis=1),
                (((1,), (1,)), ((), ())),
                preferred_element_type=F32,
            )
            result = part if result is None else result + part
        return result

    for h in (0, 1):
        for hh, _, copy in results:
            if hh == h:
                copy.wait_recv()
        rows = slice(h * BLOCK, (h + 1) * BLOCK)

        @pl.loop(0, 3)
        def _(b):
            out[pl.ds(pl.multiple_of(b * OUTB, OUTB), OUTB), rows] = ordered(h, 0, b).astype(BF16)

        out[3 * OUTB : 4 * OUTB, rows] = (ordered(h, 0, 3) + ordered(h, 1, 8)).astype(BF16)

        @pl.loop(4, 7)
        def _(b):
            out[pl.ds(pl.multiple_of(b * OUTB, OUTB), OUTB), rows] = ordered(h, 1, b).astype(BF16)

        out[7 * OUTB : D, rows] = ordered(h, 1, 7)[: D - 7 * OUTB].astype(BF16)

    sent(1)
    for own, far in shuffles:
        pl.when(jnp.logical_not(own))(far.wait_send)
    for copies in (second_0, second_1, *down_1, *down_2):
        for copy in copies[1]:
            copy.wait_send()
    for copy in tok_near + tok_far + sum(hid_near + hid_far, []) + [copy for _, _, copy in results]:
        copy.wait_send()


def body(tokens, gate_weight, up_weight, down_weight, block_counts, block_tokens):
    vmem, hbm = pl.BlockSpec(memory_space=pltpu.VMEM), pl.BlockSpec(memory_space=pltpu.HBM)
    dma = pltpu.SemaphoreType.DMA
    made = pl.pallas_call(
        kernel,
        out_shape=(
            jax.ShapeDtypeStruct((D, 2 * BLOCK), BF16),
            jax.ShapeDtypeStruct((2, 2, RING, RING, 2, 2, 48, COLS), BF16),
            jax.ShapeDtypeStruct((RING, RING, RING, 2, 48, COLS), BF16),
            jax.ShapeDtypeStruct((2, CHUNKS, RING, RING, RING, TILE, COLS), BF16),
        ),
        in_specs=[vmem, hbm, hbm, hbm, vmem, pl.BlockSpec(memory_space=pltpu.SMEM), vmem, vmem, vmem, hbm],
        out_specs=(vmem, hbm, hbm, hbm),
        scratch_shapes=[
            pltpu.VMEM((2, 2, RING, RING, 2, 2, 48, COLS), BF16),
            pltpu.VMEM((9, RING, 2, 2, PAD, COLS), BF16),
            pltpu.VMEM((RING, TOK, WIDE), BF16),
            pltpu.VMEM((2, 2, 48, 16, COLS), BF16),
            *[pltpu.VMEM((2, RING, RING, RING, TILE, COLS), BF16) for _ in range(CHUNKS)],
            pltpu.VMEM((2, TOK, COLS), BF16),
            pltpu.VMEM((RING, 2, RING, BLOCK, COLS), BF16),
            pltpu.VMEM((3, 2, CHUNKS, BLOCK, BLOCK), BF16),
            pltpu.VMEM((RING, 2, CHUNKS, BLOCK, BLOCK), BF16),
            pltpu.VMEM((BLOCK, SLOTS), jnp.int32),
            pltpu.VMEM((2, 2, TOK, COLS), F32),
            dma((2, 2, 2)),
            dma,
            dma((2, 2, RING)), dma((2, 2, RING)),
            dma((2, 2, RING, 2)), dma((2, 2, RING, 2)),
            dma((2, 2)), dma((RING,)),
            dma((2, CHUNKS, RING)), dma((2, CHUNKS, RING)),
            dma((2, CHUNKS, RING)), dma((2, CHUNKS, RING)),
            dma((RING,)), dma((RING,)),
            dma((2, RING)), dma((2, RING)),
            dma((2, CHUNKS, 3)), dma((2, CHUNKS, 3)),
        ],
        compiler_params=pltpu.CompilerParams(
            collective_id=0, has_side_effects=True, vmem_limit_bytes=60 * 2**20
        ),
    )(
        tokens.T,
        *[jnp.swapaxes(weight, 0, 1) for weight in (gate_weight, up_weight, down_weight)],
        block_tokens,
        block_counts,
        jnp.asarray(place_matrix(), BF16),
        jnp.asarray(group_matrix(), BF16),
        jnp.asarray(swap_matrix(), BF16),
        jnp.asarray(order_matrix(), BF16).reshape(9, RING, 2, 2, PAD, COLS),
    )
    return made[0].T


def solution(mesh):
    in_specs = (
        P("expert", "shard"),
        P(None, "expert", "shard"),
        P(None, "expert", "shard"),
        P(None, "expert", "shard"),
        P("expert"),
        P("expert", None),
    )
    out_specs = P(("expert", "shard"), None)
    return jax.shard_map(body, mesh=mesh, in_specs=in_specs, out_specs=out_specs, check_vma=False)
```

```python
import functools

import jax
import jax.numpy as jnp
import numpy as np
from jax import lax
from jax.experimental import pallas as pl
from jax.experimental.pallas import tpu as pltpu
from jax.sharding import PartitionSpec as P

GROUP = 32
LANES = 128
BF16 = jnp.bfloat16
F32 = jnp.float32
MESH = pl.DeviceIdType.MESH

RING = 4
D = 2880
ROWS = 90
PAD = 96
FEAT = 720
WIDE = 8 * PAD
COLS = 384
TOK = 1024
BLOCK = 256
SLOTS = 8
TILE = 16
CHUNKS = 3
OUTB = 384


def place_matrix():
    m = np.zeros((FEAT, WIDE), np.float32)
    for k in range(FEAT):
        m[k, k // ROWS * PAD + k % ROWS] = 1
    return m


def group_matrix():
    lane = np.arange(LANES) // GROUP
    return (lane[:, None] == lane[None, :]).astype(np.float32)


def swap_matrix():
    m = np.zeros((2, LANES, BLOCK), np.float32)
    for e in range(2):
        for k in range(LANES):
            m[e, k, k % 16 * 16 + k // 16 * 2 + e] = 1
    return m


def order_matrix():
    m = np.zeros((9, RING, OUTB, OUTB), np.float32)
    for d in range(D):
        pair, rest = divmod(d, 2 * ROWS)
        core, row = divmod(rest, ROWS)
        part, row = divmod(row, 48)
        chunk, row = divmod(row, TILE)
        half, pair = divmod(pair, 8)
        block, col = divmod(d, OUTB)
        if block == 3 and half == 1:
            block = 8
        m[block, 2 * core + part, col, chunk * LANES + pair * TILE + row] = 1
    return m


def power_floor(value):
    far = value * 8388609.0
    return far - (far - value)


def restore(weight, groups):
    power = power_floor(jnp.abs(weight) * 0.751953125)
    square = power * power
    sixth = (square * square) * (square * 2.0**60)
    total = jnp.dot(sixth.astype(BF16), groups, preferred_element_type=F32)
    top = power_floor(jnp.exp2((jnp.log2(total) - 60.0) * (1.0 / 6.0)) * 0.8)
    top = jnp.minimum(jnp.maximum(top, 2.0**-30), 2.0**8)
    magic = jnp.maximum(power, top * 0.25) * (1.5 * 2.0**22)
    rounded = (weight + magic) - magic
    limit = top * 1.5
    return jnp.minimum(jnp.maximum(rounded, -limit), limit).astype(BF16)


def kernel(
    tokens, gate_w, up_w, down_w, block_tokens, counts, place, groups, swap, order,
    out, mid, xs, midd, raw,
    ob, inbox, tok, stage, in_0, in_1, in_2, hid, picked, ob_out, fin, picks, shown,
    stage_sem, order_sem, shown_sem, s1_send, s1_recv, s2_send, s2_recv, xs_send, xs_recv,
    d1_send, d1_recv, d2_send, d2_recv, tok_send, tok_recv, hid_send, hid_recv, out_send, out_recv,
):
    in_d = (in_0, in_1, in_2)
    me, x = lax.axis_index("expert"), lax.axis_index("shard")
    y, z, c = me // 8, (me // 2) % 4, me % 2

    def device(yy, zz, cc, xx):
        return ((yy * 4 + zz) * 2 + cc, xx)

    def ring(at, step):
        return (at + step) % RING

    def remote(src, dst, send, recv, target):
        return pltpu.make_async_remote_copy(
            src_ref=src, dst_ref=dst, send_sem=send, recv_sem=recv, device_id=target, device_id_type=MESH
        )

    def landed(ref, sem):
        pltpu.make_async_copy(ref, ref, sem).wait()

    barrier = pltpu.get_barrier_semaphore()
    peers = [device(y, z, 1 - c, x)]
    for step in (1, 2, 3):
        for cc in (c, 1 - c):
            peers += [device(ring(y, step), z, cc, x), device(y, ring(z, step), cc, x), device(y, z, cc, ring(x, step))]
    for peer in peers:
        pl.semaphore_signal(barrier, inc=1, device_id=peer, device_id_type=MESH)

    def load(weight, yy, slot, ab):
        return pltpu.make_async_copy(
            weight.at[:, pl.ds(yy * 16, 16)], stage.at[slot, ab, 0:ROWS], stage_sem.at[slot, ab]
        )

    load(gate_w, ring(y, 1), 0, 0).start()
    load(up_w, 0, 0, 1).start()
    stage[:, :, ROWS:PAD] = jnp.zeros((2, 2, PAD - ROWS, 16, COLS), BF16)
    turned = jnp.transpose(block_tokens[...])
    for n in range(SLOTS):
        picks[n] = jnp.broadcast_to(turned[:, n : n + 1], (BLOCK, LANES))

    pl.semaphore_wait(barrier, len(peers))

    right, left = device(y, z, c, ring(x, 1)), device(y, z, c, ring(x, 3))
    tok_near = [
        remote(tokens, raw.at[x], tok_send.at[0], tok_recv.at[0], right),
        remote(tokens, raw.at[x], tok_send.at[1], tok_recv.at[1], left),
    ]
    for copy in tok_near:
        copy.start()
    lower, upper = raw.at[ring(x, 3), 0:368], raw.at[ring(x, 1), 368:FEAT]
    tok_far = [
        remote(lower, lower, tok_send.at[2], tok_recv.at[2], right),
        remote(upper, upper, tok_send.at[3], tok_recv.at[3], left),
    ]

    def encode(slot, ab, e, to):
        @pl.loop(0, 6, unroll=3)
        def _(j):
            rows = pl.ds(pl.multiple_of(j * TILE, TILE), TILE)
            for lane in range(COLS // LANES):
                cols = slice(lane * LANES, (lane + 1) * LANES)
                block = stage[slot, ab, rows, :, cols].reshape(BLOCK, LANES)
                for n in (0, 1):
                    weight = jnp.dot(swap[e, n * 64 : n * 64 + 64, :], block, preferred_element_type=F32)
                    ob[*to, 2 * n : 2 * n + 2, :, rows, cols] = restore(weight, groups[...]).reshape(2, 2, TILE, LANES)

    def first_y(q, step):
        to = ring(y, step)
        return ob.at[0, q, to], mid.at[0, q, y], s1_send.at[0, q, step], s1_recv.at[0, q, step], device(to, z, c, x)

    def first_z(q, step, yy):
        to = ring(z, step)
        send, recv = s1_send.at[1, q, step], s1_recv.at[1, q, step]
        return ob.at[1, q, yy, to], mid.at[1, q, z, yy], send, recv, device(y, to, c, x)

    @pl.loop(0, 8)
    def _(n):
        slot, q, i = n % 2, n // 4, n % 4
        load(gate_w, ring(y, i + 1), slot, 0).wait()
        load(up_w, i, slot, 1).wait()

        @pl.when(n < 7)
        def _():
            load(gate_w, ring(y, n + 2), 1 - slot, 0).start()
            load(up_w, (n + 1) % 4, 1 - slot, 1).start()

        encode(slot, 0, q, (0, q, ring(y, i + 1)))

        @pl.when(i == 3)
        def _():
            src, dst, _, recv, _ = first_y(q, 0)
            pltpu.make_async_copy(src, dst, recv).start()

        @pl.when(i != 3)
        def _():
            remote(*first_y(q, i + 1)).start()

        encode(slot, 1, q, (1, q, i))
        for step in (2, 1, 3):
            remote(*first_z(q, step, i)).start()
        src, dst, _, recv, _ = first_z(q, 0, i)
        pltpu.make_async_copy(src, dst, recv).start()

    load(down_w, 0, 0, 0).start()
    everything = slice(None)

    def second(q):
        local, far = [], []
        for step in (2, 1, 3, 0):
            for dc in (0, 1):
                cc = (c + dc) % 2
                zz, yy = ring(z, step), ring(y, step)
                a = (mid.at[0, q, :, zz, cc], inbox.at[0:4, z, c, q])
                b = (mid.at[1, q, :, yy, cc], inbox.at[4 + y, :, c, q])
                if step == 0 and dc == 0:
                    local += [pltpu.make_async_copy(*pair, s2_recv.at[ab, q, 0, 0]) for ab, pair in enumerate((a, b))]
                    continue
                for ab, pair, target in ((0, a, device(y, zz, cc, x)), (1, b, device(yy, z, cc, x))):
                    far.append(remote(*pair, s2_send.at[ab, q, step, dc], s2_recv.at[ab, q, step, dc], target))
        return local, far

    def pass_on(q):
        for step in range(RING):
            landed(mid.at[0, q, y], s1_recv.at[0, q, step])
            landed(mid.at[1, q, z], s1_recv.at[1, q, step])
        local, far = second(q)
        for copy in far + local:
            copy.start()
        return local, far

    def sent(q):
        for step in (1, 2, 3):
            remote(*first_y(q, step)).wait_send()
            remote(*first_z(q, step, everything)).wait_send()

    second_0 = pass_on(0)
    for near, far in zip(tok_near, tok_far):
        near.wait_recv()
        far.start()

    sent(0)

    @pl.loop(0, 4)
    def _(n):
        slot = n % 2
        load(down_w, n, slot, 0).wait()

        @pl.when(n < 3)
        def _():
            load(down_w, n + 1, 1 - slot, 0).start()

        for e in (0, 1):
            encode(slot, 0, e, (e, 0, n))

    shuffles = []
    for cc in (0, 1):
        for h in (0, 1):
            to = 2 * c + h
            src, dst = ob.at[:, 0, :, :, cc, 48 * h : 48 * h + 48], xs.at[x]
            own = jnp.logical_and(cc == c, to == x)
            far = remote(src, dst, xs_send.at[cc, h], xs_recv.at[x], device(y, z, cc, to))
            near = pltpu.make_async_copy(src, dst, xs_recv.at[x])
            pl.when(own)(near.start)
            pl.when(jnp.logical_not(own))(far.start)
            shuffles.append((own, far))

    second_1 = pass_on(1)

    def arrived(copies):
        local, far = copies
        for copy in local:
            copy.wait()
        for copy in far:
            copy.wait_recv()

    def show(n):
        return pltpu.make_async_copy(raw.at[ring(x, n)], shown.at[n % 2], shown_sem.at[n % 2])

    for copy in tok_far:
        copy.wait_recv()
    own_tokens = pltpu.make_async_copy(tokens, shown.at[0], shown_sem.at[0])
    own_tokens.start()
    for n in range(RING):
        if n < RING - 1:
            show(n + 1).start()
        (show(n) if n else own_tokens).wait()

        @pl.loop(0, 4)
        def _(i):
            rows = pl.ds(pl.multiple_of(i * 256, 256), 256)
            tok[ring(x, n), rows, :] = lax.dot_general(
                shown[n % 2, :, rows], place[...], (((0,), (0,)), ((), ())), preferred_element_type=F32
            ).astype(BF16)

    def products(e):
        @pl.loop(0, 4)
        def _(n):
            rows = pl.ds(pl.multiple_of(n * 256, 256), 256)
            made = []
            for ab in (0, 1):
                total = None
                for s in range(RING):
                    weight = inbox[4 * ab + s, :, :, e].reshape(WIDE, COLS)
                    part = jnp.dot(tok[s, rows, :], weight, preferred_element_type=F32)
                    total = part if total is None else total + part
                made.append(total)
            gate, up = made
            hid[x, e, rows, :] = ((up + 1.0) * gate * jax.nn.sigmoid(1.702 * gate)).astype(BF16)

    hid_near, hid_far = [], []
    for h in (0, 1):
        own, below, above = hid.at[x, h], hid.at[ring(x, 3), h, 0:512], hid.at[ring(x, 1), h, 512:TOK]
        hid_near.append([
            remote(own, own, hid_send.at[h, 0], hid_recv.at[h, 0], right),
            remote(own, own, hid_send.at[h, 1], hid_recv.at[h, 1], left),
        ])
        hid_far.append([
            remote(below, below, hid_send.at[h, 2], hid_recv.at[h, 2], right),
            remote(above, above, hid_send.at[h, 3], hid_recv.at[h, 3], left),
        ])

    arrived(second_0)
    products(0)

    for n in range(RING):
        landed(xs.at[n], xs_recv.at[n])

    def down_first(r):
        local, far = [], []
        for step in (2, 1, 3, 0):
            yy, zz = ring(y, step), ring(z, step)
            rows = pl.ds(r * TILE, TILE)
            a = (xs.at[:, 0, yy, :, rows], midd.at[0, r, :, y])
            b = (xs.at[:, 1, :, zz, rows], midd.at[1, r, :, z])
            if step == 0:
                local += [pltpu.make_async_copy(*pair, d1_recv.at[ab, r, 0]) for ab, pair in enumerate((a, b))]
                continue
            for ab, pair, target in ((0, a, device(yy, z, c, x)), (1, b, device(y, zz, c, x))):
                far.append(remote(*pair, d1_send.at[ab, r, step], d1_recv.at[ab, r, step], target))
        return local, far

    def down_second(r):
        local, far = [], []
        for step in (2, 1, 3, 0):
            yy, zz = ring(y, step), ring(z, step)
            a = (midd.at[0, r, :, :, zz], in_d[r].at[0, :, :, z])
            b = (midd.at[1, r, :, :, yy], in_d[r].at[1, :, y])
            if step == 0:
                local += [pltpu.make_async_copy(*pair, d2_recv.at[ab, r, 0]) for ab, pair in enumerate((a, b))]
                continue
            for ab, pair, target in ((0, a, device(y, zz, c, x)), (1, b, device(yy, z, c, x))):
                far.append(remote(*pair, d2_send.at[ab, r, step], d2_recv.at[ab, r, step], target))
        return local, far

    def start(copies):
        for copy in copies[1] + copies[0]:
            copy.start()

    down_1 = [down_first(r) for r in range(CHUNKS)]
    down_2 = [down_second(r) for r in range(CHUNKS)]
    for copies in down_1:
        start(copies)
    for copy in hid_near[0]:
        copy.start()

    arrived(second_1)
    products(1)
    for copy in hid_near[1]:
        copy.start()

    load_order = pltpu.make_async_copy(order, inbox, order_sem)
    load_order.start()

    def hid_forward(h):
        for near, far in zip(hid_near[h], hid_far[h]):
            near.wait_recv()
            far.start()

    arrived(down_1[0])
    start(down_2[0])
    hid_forward(0)
    arrived(down_1[1])
    start(down_2[1])
    hid_forward(1)
    arrived(down_1[2])
    start(down_2[2])

    results = []

    first, total = counts[0], counts[0] + counts[1]
    lanes = lax.broadcasted_iota(jnp.int32, (BLOCK, LANES), 1)

    def pick(h, step):
        slot = 2 * ring(x, step) + h
        row = jnp.where(slot < total, picks[slot], -1)
        chosen = jnp.concatenate([(row - n * LANES == lanes).astype(F32) for n in range(TOK // LANES)], axis=1).astype(BF16)
        which = (slot >= first).astype(jnp.int32)
        for s in range(RING):
            picked[step, s] = jnp.dot(chosen, hid[s, which], preferred_element_type=F32).astype(BF16)

    def project(h, r, step):
        to = ring(x, step)
        which = (2 * to + h >= first).astype(jnp.int32)
        made = None
        for s in range(RING):
            part = lax.dot_general(
                picked[step, s],
                in_d[r][which, s].reshape(BLOCK, COLS),
                (((1,), (1,)), ((), ())),
                preferred_element_type=F32,
            )
            made = part if made is None else made + part
        if step == 0:
            fin[x, h, r] = made.astype(BF16)
            return
        ob_out[step - 1, h, r] = made.astype(BF16)
        copy = remote(
            ob_out.at[step - 1, h, r], fin.at[x, h, r], out_send.at[h, r, step - 1], out_recv.at[h, r, step - 1],
            device(y, z, c, to),
        )
        copy.start()
        results.append((h, r, copy))

    for copy in hid_far[0] + hid_far[1]:
        copy.wait_recv()
    arrived(down_2[0])
    for step in (2, 1, 3, 0):
        pick(0, step)
        project(0, 0, step)
    arrived(down_2[1])
    for step in (2, 1, 3, 0):
        project(0, 1, step)
    arrived(down_2[2])
    for step in (2, 1, 3, 0):
        project(0, 2, step)
    for step in (2, 1, 3, 0):
        pick(1, step)
        for r in range(CHUNKS):
            project(1, r, step)

    load_order.wait()

    def ordered(h, half, matrix):
        result = None
        table = inbox[matrix].reshape(RING * OUTB, OUTB)
        for n in range(RING):
            got = [fin[n, h, r, :, half * LANES : (half + 1) * LANES] for r in range(CHUNKS)]
            part = lax.dot_general(
                table[n * OUTB : (n + 1) * OUTB],
                jnp.concatenate(got, axis=1),
                (((1,), (1,)), ((), ())),
                preferred_element_type=F32,
            )
            result = part if result is None else result + part
        return result

    for h in (0, 1):
        for hh, _, copy in results:
            if hh == h:
                copy.wait_recv()
        rows = slice(h * BLOCK, (h + 1) * BLOCK)

        @pl.loop(0, 3)
        def _(b):
            out[pl.ds(pl.multiple_of(b * OUTB, OUTB), OUTB), rows] = ordered(h, 0, b).astype(BF16)

        out[3 * OUTB : 4 * OUTB, rows] = (ordered(h, 0, 3) + ordered(h, 1, 8)).astype(BF16)

        @pl.loop(4, 7)
        def _(b):
            out[pl.ds(pl.multiple_of(b * OUTB, OUTB), OUTB), rows] = ordered(h, 1, b).astype(BF16)

        out[7 * OUTB : D, rows] = ordered(h, 1, 7)[: D - 7 * OUTB].astype(BF16)

    sent(1)
    for own, far in shuffles:
        pl.when(jnp.logical_not(own))(far.wait_send)
    for copies in (second_0, second_1, *down_1, *down_2):
        for copy in copies[1]:
            copy.wait_send()
    for copy in tok_near + tok_far + sum(hid_near + hid_far, []) + [copy for _, _, copy in results]:
        copy.wait_send()


def body(tokens, gate_weight, up_weight, down_weight, block_counts, block_tokens):
    vmem, hbm = pl.BlockSpec(memory_space=pltpu.VMEM), pl.BlockSpec(memory_space=pltpu.HBM)
    dma = pltpu.SemaphoreType.DMA
    made = pl.pallas_call(
        kernel,
        out_shape=(
            jax.ShapeDtypeStruct((D, 2 * BLOCK), BF16),
            jax.ShapeDtypeStruct((2, 2, RING, RING, 2, PAD, COLS), BF16),
            jax.ShapeDtypeStruct((RING, 2, RING, RING, 48, COLS), BF16),
            jax.ShapeDtypeStruct((2, CHUNKS, RING, RING, RING, TILE, COLS), BF16),
            jax.ShapeDtypeStruct((RING, FEAT, TOK), BF16),
        ),
        in_specs=[hbm, hbm, hbm, hbm, vmem, pl.BlockSpec(memory_space=pltpu.SMEM), vmem, vmem, vmem, hbm],
        out_specs=(vmem, hbm, hbm, hbm, hbm),
        scratch_shapes=[
            pltpu.VMEM((2, 2, RING, RING, 2, PAD, COLS), BF16),
            pltpu.VMEM((9, RING, 2, 2, PAD, COLS), BF16),
            pltpu.VMEM((RING, TOK, WIDE), BF16),
            pltpu.VMEM((2, 2, PAD, 16, COLS), BF16),
            *[pltpu.VMEM((2, RING, RING, RING, TILE, COLS), BF16) for _ in range(CHUNKS)],
            pltpu.VMEM((RING, 2, TOK, COLS), BF16),
            pltpu.VMEM((RING, RING, BLOCK, COLS), BF16),
            pltpu.VMEM((3, 2, CHUNKS, BLOCK, BLOCK), BF16),
            pltpu.VMEM((RING, 2, CHUNKS, BLOCK, BLOCK), BF16),
            pltpu.VMEM((SLOTS, BLOCK, LANES), jnp.int32),
            pltpu.VMEM((2, FEAT, TOK), BF16),
            dma((2, 2)),
            dma,
            dma((2,)),
            dma((2, 2, RING)), dma((2, 2, RING)),
            dma((2, 2, RING, 2)), dma((2, 2, RING, 2)),
            dma((2, 2)), dma((RING,)),
            dma((2, CHUNKS, RING)), dma((2, CHUNKS, RING)),
            dma((2, CHUNKS, RING)), dma((2, CHUNKS, RING)),
            dma((RING,)), dma((RING,)),
            dma((2, RING)), dma((2, RING)),
            dma((2, CHUNKS, 3)), dma((2, CHUNKS, 3)),
        ],
        compiler_params=pltpu.CompilerParams(
            collective_id=0, has_side_effects=True, vmem_limit_bytes=60 * 2**20
        ),
    )(
        tokens.T,
        *[jnp.swapaxes(weight, 0, 1) for weight in (gate_weight, up_weight, down_weight)],
        block_tokens,
        block_counts,
        jnp.asarray(place_matrix(), BF16),
        jnp.asarray(group_matrix(), BF16),
        jnp.asarray(swap_matrix(), BF16),
        jnp.asarray(order_matrix(), BF16).reshape(9, RING, 2, 2, PAD, COLS),
    )
    return made[0].T


def solution(mesh):
    in_specs = (
        P("expert", "shard"),
        P(None, "expert", "shard"),
        P(None, "expert", "shard"),
        P(None, "expert", "shard"),
        P("expert"),
        P("expert", None),
    )
    out_specs = P(("expert", "shard"), None)
    return jax.shard_map(body, mesh=mesh, in_specs=in_specs, out_specs=out_specs, check_vma=False)
```

```python
import functools

import jax
import jax.numpy as jnp
import numpy as np
from jax import lax
from jax.experimental import pallas as pl
from jax.experimental.pallas import tpu as pltpu
from jax.sharding import PartitionSpec as P

GROUP = 32
LANES = 128
BF16 = jnp.bfloat16
F32 = jnp.float32
MESH = pl.DeviceIdType.MESH

RING = 4
D = 2880
ROWS = 90
PAD = 96
FEAT = 720
WIDE = 8 * PAD
COLS = 384
TOK = 1024
BLOCK = 256
SLOTS = 8
TILE = 16
CHUNKS = 3
OUTB = 384


def place_matrix():
    m = np.zeros((FEAT, WIDE), np.float32)
    for k in range(FEAT):
        m[k, k // ROWS * PAD + k % ROWS] = 1
    return m


def group_matrix():
    lane = np.arange(LANES) // GROUP
    return (lane[:, None] == lane[None, :]).astype(np.float32)


def swap_matrix():
    m = np.zeros((2, LANES, BLOCK), np.float32)
    for e in range(2):
        for k in range(LANES):
            m[e, k, k % 16 * 16 + k // 16 * 2 + e] = 1
    return m


def order_matrix():
    m = np.zeros((9, RING, OUTB, OUTB), np.float32)
    for d in range(D):
        pair, rest = divmod(d, 2 * ROWS)
        core, row = divmod(rest, ROWS)
        part, row = divmod(row, 48)
        chunk, row = divmod(row, TILE)
        half, pair = divmod(pair, 8)
        block, col = divmod(d, OUTB)
        if block == 3 and half == 1:
            block = 8
        m[block, 2 * core + part, col, chunk * LANES + pair * TILE + row] = 1
    return m


def power_floor(value):
    far = value * 8388609.0
    return far - (far - value)


def restore(weight, groups):
    power = power_floor(jnp.abs(weight) * 0.751953125)
    square = power * power
    sixth = (square * square) * (square * 2.0**60)
    total = jnp.dot(sixth.astype(BF16), groups, preferred_element_type=F32)
    top = power_floor(jnp.exp2((jnp.log2(total) - 60.0) * (1.0 / 6.0)) * 0.8)
    top = jnp.minimum(jnp.maximum(top, 2.0**-30), 2.0**8)
    magic = jnp.maximum(power, top * 0.25) * (1.5 * 2.0**22)
    rounded = (weight + magic) - magic
    limit = top * 1.5
    return jnp.minimum(jnp.maximum(rounded, -limit), limit).astype(BF16)


def kernel(
    tokens, gate_w, up_w, down_w, block_tokens, counts, place, groups, swap, order,
    out, mid, xs, midd, raw,
    ob, inbox, tok, stage, in_0, in_1, in_2, hid_0, hid_1, hid_2, hid_3, ob_out, fin, picks, shown, made_out,
    stage_sem, order_sem, shown_sem, made_sem, s1_send, s1_recv, s2_send, s2_recv, xs_send, xs_recv,
    d1_send, d1_recv, d2_send, d2_recv, tok_send, tok_recv, hid_send, hid_recv, out_send, out_recv,
):
    in_d = (in_0, in_1, in_2)
    hid = (hid_0, hid_1, hid_2, hid_3)
    me, x = lax.axis_index("expert"), lax.axis_index("shard")
    y, z, c = me // 8, (me // 2) % 4, me % 2

    def device(yy, zz, cc, xx):
        return ((yy * 4 + zz) * 2 + cc, xx)

    def ring(at, step):
        return (at + step) % RING

    def remote(src, dst, send, recv, target):
        return pltpu.make_async_remote_copy(
            src_ref=src, dst_ref=dst, send_sem=send, recv_sem=recv, device_id=target, device_id_type=MESH
        )

    def landed(ref, sem):
        pltpu.make_async_copy(ref, ref, sem).wait()

    barrier = pltpu.get_barrier_semaphore()
    peers = [device(y, z, 1 - c, x)]
    for step in (1, 2, 3):
        for cc in (c, 1 - c):
            peers += [device(ring(y, step), z, cc, x), device(y, ring(z, step), cc, x), device(y, z, cc, ring(x, step))]
    for peer in peers:
        pl.semaphore_signal(barrier, inc=1, device_id=peer, device_id_type=MESH)

    def load(weight, yy, slot, ab):
        return pltpu.make_async_copy(
            weight.at[:, pl.ds(yy * 16, 16)], stage.at[slot, ab, 0:ROWS], stage_sem.at[slot, ab]
        )

    load(gate_w, ring(y, 1), 0, 0).start()
    load(up_w, 0, 0, 1).start()
    stage[:, :, ROWS:PAD] = jnp.zeros((2, 2, PAD - ROWS, 16, COLS), BF16)
    turned = jnp.transpose(block_tokens[...])
    for n in range(SLOTS):
        picks[n] = jnp.broadcast_to(turned[:, n : n + 1], (BLOCK, LANES))

    pl.semaphore_wait(barrier, len(peers))

    right, left = device(y, z, c, ring(x, 1)), device(y, z, c, ring(x, 3))
    tok_near = [
        remote(tokens, raw.at[x], tok_send.at[0], tok_recv.at[0], right),
        remote(tokens, raw.at[x], tok_send.at[1], tok_recv.at[1], left),
    ]
    for copy in tok_near:
        copy.start()
    lower, upper = raw.at[ring(x, 3), 0:368], raw.at[ring(x, 1), 368:FEAT]
    tok_far = [
        remote(lower, lower, tok_send.at[2], tok_recv.at[2], right),
        remote(upper, upper, tok_send.at[3], tok_recv.at[3], left),
    ]

    def encode(slot, ab, e, to):
        @pl.loop(0, 6, unroll=3)
        def _(j):
            rows = pl.ds(pl.multiple_of(j * TILE, TILE), TILE)
            for lane in range(COLS // LANES):
                cols = slice(lane * LANES, (lane + 1) * LANES)
                block = stage[slot, ab, rows, :, cols].reshape(BLOCK, LANES)
                for n in (0, 1):
                    weight = jnp.dot(swap[e, n * 64 : n * 64 + 64, :], block, preferred_element_type=F32)
                    ob[*to, 2 * n : 2 * n + 2, :, rows, cols] = restore(weight, groups[...]).reshape(2, 2, TILE, LANES)

    def first_y(q, step):
        to = ring(y, step)
        return ob.at[0, q, to], mid.at[0, q, y], s1_send.at[0, q, step], s1_recv.at[0, q, step], device(to, z, c, x)

    def first_z(q, step, yy):
        to = ring(z, step)
        send, recv = s1_send.at[1, q, step], s1_recv.at[1, q, step]
        return ob.at[1, q, yy, to], mid.at[1, q, z, yy], send, recv, device(y, to, c, x)

    @pl.loop(0, 8)
    def _(n):
        slot, q, i = n % 2, n // 4, n % 4
        load(gate_w, ring(y, i + 1), slot, 0).wait()
        load(up_w, i, slot, 1).wait()

        @pl.when(n < 7)
        def _():
            load(gate_w, ring(y, n + 2), 1 - slot, 0).start()
            load(up_w, (n + 1) % 4, 1 - slot, 1).start()

        encode(slot, 0, q, (0, q, ring(y, i + 1)))

        @pl.when(i == 3)
        def _():
            src, dst, _, recv, _ = first_y(q, 0)
            pltpu.make_async_copy(src, dst, recv).start()

        @pl.when(i != 3)
        def _():
            remote(*first_y(q, i + 1)).start()

        encode(slot, 1, q, (1, q, i))
        for step in (2, 1, 3):
            remote(*first_z(q, step, i)).start()
        src, dst, _, recv, _ = first_z(q, 0, i)
        pltpu.make_async_copy(src, dst, recv).start()

    load(down_w, 0, 0, 0).start()
    everything = slice(None)

    def second(q):
        local, far = [], []
        for step in (2, 1, 3, 0):
            for dc in (0, 1):
                cc = (c + dc) % 2
                zz, yy = ring(z, step), ring(y, step)
                a = (mid.at[0, q, :, zz, cc], inbox.at[0:4, z, c, q])
                b = (mid.at[1, q, :, yy, cc], inbox.at[4 + y, :, c, q])
                if step == 0 and dc == 0:
                    local += [pltpu.make_async_copy(*pair, s2_recv.at[ab, q, 0, 0]) for ab, pair in enumerate((a, b))]
                    continue
                for ab, pair, target in ((0, a, device(y, zz, cc, x)), (1, b, device(yy, z, cc, x))):
                    far.append(remote(*pair, s2_send.at[ab, q, step, dc], s2_recv.at[ab, q, step, dc], target))
        return local, far

    def pass_on(q):
        for step in range(RING):
            landed(mid.at[0, q, y], s1_recv.at[0, q, step])
            landed(mid.at[1, q, z], s1_recv.at[1, q, step])
        local, far = second(q)
        for copy in far + local:
            copy.start()
        return local, far

    def sent(q):
        for step in (1, 2, 3):
            remote(*first_y(q, step)).wait_send()
            remote(*first_z(q, step, everything)).wait_send()

    second_0 = pass_on(0)
    for near, far in zip(tok_near, tok_far):
        near.wait_recv()
        far.start()

    def shuffle(cc, h, yy):
        to = 2 * c + h
        src, dst = ob.at[:, 0, yy, :, cc, 48 * h : 48 * h + 48], xs.at[x, :, yy]
        far = remote(src, dst, xs_send.at[cc, h], xs_recv.at[x], device(y, z, cc, to))
        near = pltpu.make_async_copy(src, dst, xs_recv.at[x])
        return jnp.logical_and(cc == c, to == x), near, far

    sent(0)

    @pl.loop(0, 4)
    def _(n):
        slot = n % 2
        load(down_w, n, slot, 0).wait()

        @pl.when(n < 3)
        def _():
            load(down_w, n + 1, 1 - slot, 0).start()

        for e in (0, 1):
            encode(slot, 0, e, (e, 0, n))
        for cc in (0, 1):
            for h in (0, 1):
                own, near, far = shuffle(cc, h, n)
                pl.when(own)(near.start)
                pl.when(jnp.logical_not(own))(far.start)

    second_1 = pass_on(1)

    def arrived(copies):
        local, far = copies
        for copy in local:
            copy.wait()
        for copy in far:
            copy.wait_recv()

    def show(n):
        return pltpu.make_async_copy(raw.at[ring(x, n)], shown.at[n % 2], shown_sem.at[n % 2])

    for copy in tok_far:
        copy.wait_recv()
    own_tokens = pltpu.make_async_copy(tokens, shown.at[0], shown_sem.at[0])
    own_tokens.start()
    for n in range(RING):
        if n < RING - 1:
            show(n + 1).start()
        (show(n) if n else own_tokens).wait()

        @pl.loop(0, 4)
        def _(i):
            rows = pl.ds(pl.multiple_of(i * 256, 256), 256)
            tok[ring(x, n), rows, :] = lax.dot_general(
                shown[n % 2, :, rows], place[...], (((0,), (0,)), ((), ())), preferred_element_type=F32
            ).astype(BF16)

    def products(e):
        @pl.loop(0, 4)
        def _(n):
            rows = pl.ds(pl.multiple_of(n * 256, 256), 256)
            made = []
            for ab in (0, 1):
                total = None
                for s in range(RING):
                    weight = inbox[4 * ab + s, :, :, e].reshape(WIDE, COLS)
                    part = jnp.dot(tok[s, rows, :], weight, preferred_element_type=F32)
                    total = part if total is None else total + part
                made.append(total)
            gate, up = made
            hid_0[e, rows, :] = ((up + 1.0) * gate * jax.nn.sigmoid(1.702 * gate)).astype(BF16)

    hid_near, hid_far = [], []
    low, high = slice(0, 512), slice(512, TOK)
    for e in (0, 1):
        hid_near.append([
            remote(hid_0.at[e], hid_1.at[e], hid_send.at[e, 0], hid_recv.at[e, 0], right),
            remote(hid_0.at[e], hid_2.at[e], hid_send.at[e, 1], hid_recv.at[e, 1], left),
        ])
        hid_far.append([
            remote(hid_1.at[e, low], hid_3.at[e, low], hid_send.at[e, 2], hid_recv.at[e, 2], right),
            remote(hid_2.at[e, high], hid_3.at[e, high], hid_send.at[e, 3], hid_recv.at[e, 3], left),
        ])

    arrived(second_0)
    products(0)
    for copy in hid_near[0]:
        copy.start()

    for n in range(RING):
        landed(xs.at[n], xs_recv.at[n])

    def down_first(r):
        local, far = [], []
        for step in (2, 1, 3, 0):
            yy, zz = ring(y, step), ring(z, step)
            rows = pl.ds(r * TILE, TILE)
            a = (xs.at[:, 0, yy, :, rows], midd.at[0, r, :, y])
            b = (xs.at[:, 1, :, zz, rows], midd.at[1, r, :, z])
            if step == 0:
                local += [pltpu.make_async_copy(*pair, d1_recv.at[ab, r, 0]) for ab, pair in enumerate((a, b))]
                continue
            for ab, pair, target in ((0, a, device(yy, z, c, x)), (1, b, device(y, zz, c, x))):
                far.append(remote(*pair, d1_send.at[ab, r, step], d1_recv.at[ab, r, step], target))
        return local, far

    def down_second(r):
        local, far = [], []
        for step in (2, 1, 3, 0):
            yy, zz = ring(y, step), ring(z, step)
            a = (midd.at[0, r, :, :, zz], in_d[r].at[0, :, :, z])
            b = (midd.at[1, r, :, :, yy], in_d[r].at[1, :, y])
            if step == 0:
                local += [pltpu.make_async_copy(*pair, d2_recv.at[ab, r, 0]) for ab, pair in enumerate((a, b))]
                continue
            for ab, pair, target in ((0, a, device(y, zz, c, x)), (1, b, device(yy, z, c, x))):
                far.append(remote(*pair, d2_send.at[ab, r, step], d2_recv.at[ab, r, step], target))
        return local, far

    def start(copies):
        for copy in copies[1] + copies[0]:
            copy.start()

    down_1 = [down_first(r) for r in range(CHUNKS)]
    down_2 = [down_second(r) for r in range(CHUNKS)]
    for copies in down_1:
        start(copies)

    arrived(second_1)
    products(1)
    for copy in hid_near[1]:
        copy.start()

    load_order = pltpu.make_async_copy(order, inbox, order_sem)
    load_order.start()

    def hid_forward(h):
        for near, far in zip(hid_near[h], hid_far[h]):
            near.wait_recv()
            far.start()

    arrived(down_1[0])
    start(down_2[0])
    hid_forward(0)
    arrived(down_1[1])
    start(down_2[1])
    hid_forward(1)
    arrived(down_1[2])
    start(down_2[2])

    results = []

    first, total = counts[0], counts[0] + counts[1]
    lanes = lax.broadcasted_iota(jnp.int32, (BLOCK, LANES), 1)

    def kept(h, step, n):
        return step, slice(n * BLOCK, (n + 1) * BLOCK), slice(h * COLS, (h + 1) * COLS)

    def pick(h, step, shards):
        slot = 2 * ring(x, step) + h
        row = jnp.where(slot < total, picks[slot], -1)
        chosen = jnp.concatenate([(row - n * LANES == lanes).astype(F32) for n in range(TOK // LANES)], axis=1).astype(BF16)
        which = (slot >= first).astype(jnp.int32)
        for n in shards:
            tok[kept(h, step, n)] = jnp.dot(chosen, hid[n][which], preferred_element_type=F32).astype(BF16)

    def project(h, r, step):
        to = ring(x, step)
        which = (2 * to + h >= first).astype(jnp.int32)
        made = None
        for n, away in enumerate((0, 3, 1, 2)):
            part = lax.dot_general(
                tok[kept(h, step, n)],
                in_d[r][which, ring(x, away)].reshape(BLOCK, COLS),
                (((1,), (1,)), ((), ())),
                preferred_element_type=F32,
            )
            made = part if made is None else made + part
        if step == 0:
            fin[x, h, r] = made.astype(BF16)
            return
        ob_out[step - 1, h, r] = made.astype(BF16)
        copy = remote(
            ob_out.at[step - 1, h, r], fin.at[x, h, r], out_send.at[h, r, step - 1], out_recv.at[h, r, step - 1],
            device(y, z, c, to),
        )
        copy.start()
        results.append((h, r, copy))

    for step in (2, 1, 3, 0):
        pick(0, step, (0, 1, 2))
    arrived(down_2[0])
    for copy in hid_far[0] + hid_far[1]:
        copy.wait_recv()
    for step in (2, 1, 3, 0):
        pick(0, step, (3,))
        project(0, 0, step)
    arrived(down_2[1])
    for step in (2, 1, 3, 0):
        project(0, 1, step)
    for step in (2, 1, 3, 0):
        pick(1, step, (0, 1, 2, 3))
        project(1, 0, step)
        project(1, 1, step)
    arrived(down_2[2])
    for h in (0, 1):
        for step in (2, 1, 3, 0):
            project(h, 2, step)

    load_order.wait()

    def ordered(h, half, matrix):
        result = None
        table = inbox[matrix].reshape(RING * OUTB, OUTB)
        for n in range(RING):
            got = [fin[n, h, r, :, half * LANES : (half + 1) * LANES] for r in range(CHUNKS)]
            part = lax.dot_general(
                table[n * OUTB : (n + 1) * OUTB],
                jnp.concatenate(got, axis=1),
                (((1,), (1,)), ((), ())),
                preferred_element_type=F32,
            )
            result = part if result is None else result + part
        return result

    def keep(b, h):
        rows = pl.ds(pl.multiple_of(b * OUTB, OUTB), OUTB) if not isinstance(b, int) else pl.ds(b * OUTB, min(OUTB, D - b * OUTB))
        spot = (rows, slice(h * BLOCK, (h + 1) * BLOCK))
        return spot, pltpu.make_async_copy(made_out.at[spot], out.at[spot], made_sem.at[h, b])

    def store(b, h, value):
        spot, copy = keep(b, h)
        made_out[spot] = value.astype(BF16)
        copy.start()

    for h in (0, 1):
        for hh, _, copy in results:
            if hh == h:
                copy.wait_recv()

        @pl.loop(0, 3)
        def _(b):
            store(b, h, ordered(h, 0, b))

        store(3, h, ordered(h, 0, 3) + ordered(h, 1, 8))

        @pl.loop(4, 7)
        def _(b):
            store(b, h, ordered(h, 1, b))

        store(7, h, ordered(h, 1, 7)[: D - 7 * OUTB])

    sent(1)
    for cc in (0, 1):
        for h in (0, 1):
            own, _, far = shuffle(cc, h, everything)
            pl.when(jnp.logical_not(own))(far.wait_send)
    for copies in (second_0, second_1, *down_1, *down_2):
        for copy in copies[1]:
            copy.wait_send()
    for h in (0, 1):
        for b in range(8):
            keep(b, h)[1].wait()
    for copy in tok_near + tok_far + sum(hid_near + hid_far, []) + [copy for _, _, copy in results]:
        copy.wait_send()


def body(tokens, gate_weight, up_weight, down_weight, block_counts, block_tokens):
    vmem, hbm = pl.BlockSpec(memory_space=pltpu.VMEM), pl.BlockSpec(memory_space=pltpu.HBM)
    dma = pltpu.SemaphoreType.DMA
    made = pl.pallas_call(
        kernel,
        out_shape=(
            jax.ShapeDtypeStruct((D, 2 * BLOCK), BF16),
            jax.ShapeDtypeStruct((2, 2, RING, RING, 2, PAD, COLS), BF16),
            jax.ShapeDtypeStruct((RING, 2, RING, RING, 48, COLS), BF16),
            jax.ShapeDtypeStruct((2, CHUNKS, RING, RING, RING, TILE, COLS), BF16),
            jax.ShapeDtypeStruct((RING, FEAT, TOK), BF16),
        ),
        in_specs=[hbm, hbm, hbm, hbm, vmem, pl.BlockSpec(memory_space=pltpu.SMEM), vmem, vmem, vmem, hbm],
        out_specs=(hbm, hbm, hbm, hbm, hbm),
        scratch_shapes=[
            pltpu.VMEM((2, 2, RING, RING, 2, PAD, COLS), BF16),
            pltpu.VMEM((9, RING, 2, 2, PAD, COLS), BF16),
            pltpu.VMEM((RING, TOK, WIDE), BF16),
            pltpu.VMEM((2, 2, PAD, 16, COLS), BF16),
            *[pltpu.VMEM((2, RING, RING, RING, TILE, COLS), BF16) for _ in range(CHUNKS)],
            *[pltpu.VMEM((2, TOK, COLS), BF16) for _ in range(RING)],
            pltpu.VMEM((3, 2, CHUNKS, BLOCK, BLOCK), BF16),
            pltpu.VMEM((RING, 2, CHUNKS, BLOCK, BLOCK), BF16),
            pltpu.VMEM((SLOTS, BLOCK, LANES), jnp.int32),
            pltpu.VMEM((2, FEAT, TOK), BF16),
            pltpu.VMEM((D, 2 * BLOCK), BF16),
            dma((2, 2)),
            dma,
            dma((2,)),
            dma((2, 8)),
            dma((2, 2, RING)), dma((2, 2, RING)),
            dma((2, 2, RING, 2)), dma((2, 2, RING, 2)),
            dma((2, 2)), dma((RING,)),
            dma((2, CHUNKS, RING)), dma((2, CHUNKS, RING)),
            dma((2, CHUNKS, RING)), dma((2, CHUNKS, RING)),
            dma((RING,)), dma((RING,)),
            dma((2, RING)), dma((2, RING)),
            dma((2, CHUNKS, 3)), dma((2, CHUNKS, 3)),
        ],
        compiler_params=pltpu.CompilerParams(
            collective_id=0, has_side_effects=True, vmem_limit_bytes=60 * 2**20
        ),
    )(
        tokens.T,
        *[jnp.swapaxes(weight, 0, 1) for weight in (gate_weight, up_weight, down_weight)],
        block_tokens,
        block_counts,
        jnp.asarray(place_matrix(), BF16),
        jnp.asarray(group_matrix(), BF16),
        jnp.asarray(swap_matrix(), BF16),
        jnp.asarray(order_matrix(), BF16).reshape(9, RING, 2, 2, PAD, COLS),
    )
    return made[0].T


def solution(mesh):
    in_specs = (
        P("expert", "shard"),
        P(None, "expert", "shard"),
        P(None, "expert", "shard"),
        P(None, "expert", "shard"),
        P("expert"),
        P("expert", None),
    )
    out_specs = P(("expert", "shard"), None)
    return jax.shard_map(body, mesh=mesh, in_specs=in_specs, out_specs=out_specs, check_vma=False)
```

```python
import functools

import jax
import jax.numpy as jnp
import numpy as np
from jax import lax
from jax.experimental import pallas as pl
from jax.experimental.pallas import tpu as pltpu
from jax.sharding import PartitionSpec as P

GROUP = 32
LANES = 128
BF16 = jnp.bfloat16
F32 = jnp.float32
MESH = pl.DeviceIdType.MESH

RING = 4
D = 2880
ROWS = 90
PAD = 96
FEAT = 720
WIDE = 8 * PAD
COLS = 384
TOK = 1024
BLOCK = 256
SLOTS = 8
TILE = 16
CHUNKS = 3
OUTB = 384


def place_matrix():
    m = np.zeros((FEAT, WIDE), np.float32)
    for k in range(FEAT):
        m[k, k // ROWS * PAD + k % ROWS] = 1
    return m


def group_matrix():
    lane = np.arange(LANES) // GROUP
    return (lane[:, None] == lane[None, :]).astype(np.float32)


def swap_matrix():
    m = np.zeros((2, LANES, BLOCK), np.float32)
    for e in range(2):
        for k in range(LANES):
            m[e, k, k % 16 * 16 + k // 16 * 2 + e] = 1
    return m


def order_matrix():
    m = np.zeros((9, RING, OUTB, OUTB), np.float32)
    for d in range(D):
        pair, rest = divmod(d, 2 * ROWS)
        core, row = divmod(rest, ROWS)
        part, row = divmod(row, 48)
        chunk, row = divmod(row, TILE)
        half, pair = divmod(pair, 8)
        block, col = divmod(d, OUTB)
        if block == 3 and half == 1:
            block = 8
        m[block, 2 * core + part, col, chunk * LANES + pair * TILE + row] = 1
    return m


def power_floor(value):
    far = value * 8388609.0
    return far - (far - value)


def restore(weight, groups):
    power = power_floor(jnp.abs(weight) * 0.751953125)
    square = power * power
    sixth = (square * square) * (square * 2.0**60)
    total = jnp.dot(sixth.astype(BF16), groups, preferred_element_type=F32)
    top = power_floor(jnp.exp2((jnp.log2(total) - 60.0) * (1.0 / 6.0)) * 0.8)
    top = jnp.minimum(jnp.maximum(top, 2.0**-30), 2.0**8)
    magic = jnp.maximum(power, top * 0.25) * (1.5 * 2.0**22)
    rounded = (weight + magic) - magic
    limit = top * 1.5
    return jnp.minimum(jnp.maximum(rounded, -limit), limit).astype(BF16)


def kernel(
    tokens, gate_w, up_w, down_w, block_tokens, counts, place, groups, swap, order,
    out, mid, xs, midd, raw,
    ob, inbox, tok, stage, in_0, in_1, in_2, hid_0, hid_1, hid_2, hid_3, ob_out, fin, picks, shown, made_out,
    stage_sem, order_sem, shown_sem, made_sem, s1_send, s1_recv, s2_send, s2_recv, xs_send, xs_recv,
    d1_send, d1_recv, d2_send, d2_recv, tok_send, tok_recv, hid_send, hid_recv, out_send, out_recv,
):
    in_d = (in_0, in_1, in_2)
    hid = (hid_0, hid_1, hid_2, hid_3)
    me, x = lax.axis_index("expert"), lax.axis_index("shard")
    y, z, c = me // 8, (me // 2) % 4, me % 2

    def device(yy, zz, cc, xx):
        return ((yy * 4 + zz) * 2 + cc, xx)

    def ring(at, step):
        return (at + step) % RING

    def remote(src, dst, send, recv, target):
        return pltpu.make_async_remote_copy(
            src_ref=src, dst_ref=dst, send_sem=send, recv_sem=recv, device_id=target, device_id_type=MESH
        )

    def landed(ref, sem):
        pltpu.make_async_copy(ref, ref, sem).wait()

    barrier = pltpu.get_barrier_semaphore()
    peers = [device(y, z, 1 - c, x)]
    for step in (1, 2, 3):
        for cc in (c, 1 - c):
            peers += [device(ring(y, step), z, cc, x), device(y, ring(z, step), cc, x), device(y, z, cc, ring(x, step))]
    for peer in peers:
        pl.semaphore_signal(barrier, inc=1, device_id=peer, device_id_type=MESH)

    def load(weight, yy, slot, ab):
        return pltpu.make_async_copy(
            weight.at[:, pl.ds(yy * 16, 16)], stage.at[slot, ab, 0:ROWS], stage_sem.at[slot, ab]
        )

    load(gate_w, ring(y, 1), 0, 0).start()
    load(up_w, 0, 0, 1).start()
    pl.semaphore_wait(barrier, len(peers))

    right, left = device(y, z, c, ring(x, 1)), device(y, z, c, ring(x, 3))
    tok_near = [
        remote(tokens, raw.at[x], tok_send.at[0], tok_recv.at[0], right),
        remote(tokens, raw.at[x], tok_send.at[1], tok_recv.at[1], left),
    ]
    for copy in tok_near:
        copy.start()
    lower, upper = raw.at[ring(x, 3), 0:368], raw.at[ring(x, 1), 368:FEAT]
    tok_far = [
        remote(lower, lower, tok_send.at[2], tok_recv.at[2], right),
        remote(upper, upper, tok_send.at[3], tok_recv.at[3], left),
    ]

    stage[:, :, ROWS:PAD] = jnp.zeros((2, 2, PAD - ROWS, 16, COLS), BF16)

    def encode(slot, ab, e, to):
        @pl.loop(0, 6, unroll=3)
        def _(j):
            rows = pl.ds(pl.multiple_of(j * TILE, TILE), TILE)
            for lane in range(COLS // LANES):
                cols = slice(lane * LANES, (lane + 1) * LANES)
                block = stage[slot, ab, rows, :, cols].reshape(BLOCK, LANES)
                for n in (0, 1):
                    weight = jnp.dot(swap[e, n * 64 : n * 64 + 64, :], block, preferred_element_type=F32)
                    ob[*to, 2 * n : 2 * n + 2, :, rows, cols] = restore(weight, groups[...]).reshape(2, 2, TILE, LANES)

    def first_y(q, step):
        to = ring(y, step)
        return ob.at[0, q, to], mid.at[0, q, y], s1_send.at[0, q, step], s1_recv.at[0, q, step], device(to, z, c, x)

    def first_z(q, step, yy):
        to = ring(z, step)
        send, recv = s1_send.at[1, q, step], s1_recv.at[1, q, step]
        return ob.at[1, q, yy, to], mid.at[1, q, z, yy], send, recv, device(y, to, c, x)

    @pl.loop(0, 8)
    def _(n):
        slot, q, i = n % 2, n // 4, n % 4
        load(gate_w, ring(y, i + 1), slot, 0).wait()
        load(up_w, i, slot, 1).wait()

        @pl.when(n < 7)
        def _():
            load(gate_w, ring(y, n + 2), 1 - slot, 0).start()
            load(up_w, (n + 1) % 4, 1 - slot, 1).start()

        encode(slot, 0, q, (0, q, ring(y, i + 1)))

        @pl.when(i == 3)
        def _():
            src, dst, _, recv, _ = first_y(q, 0)
            pltpu.make_async_copy(src, dst, recv).start()

        @pl.when(i != 3)
        def _():
            remote(*first_y(q, i + 1)).start()

        encode(slot, 1, q, (1, q, i))
        for step in (2, 1, 3):
            remote(*first_z(q, step, i)).start()
        src, dst, _, recv, _ = first_z(q, 0, i)
        pltpu.make_async_copy(src, dst, recv).start()

    load(down_w, 0, 0, 0).start()
    everything = slice(None)

    def second(q):
        local, far = [], []
        for step in (2, 1, 3, 0):
            for dc in (0, 1):
                cc = (c + dc) % 2
                zz, yy = ring(z, step), ring(y, step)
                a = (mid.at[0, q, :, zz, cc], inbox.at[0:4, z, c, q])
                b = (mid.at[1, q, :, yy, cc], inbox.at[4 + y, :, c, q])
                if step == 0 and dc == 0:
                    local += [pltpu.make_async_copy(*pair, s2_recv.at[ab, q, 0, 0]) for ab, pair in enumerate((a, b))]
                    continue
                for ab, pair, target in ((0, a, device(y, zz, cc, x)), (1, b, device(yy, z, cc, x))):
                    far.append(remote(*pair, s2_send.at[ab, q, step, dc], s2_recv.at[ab, q, step, dc], target))
        return local, far

    def pass_on(q):
        for step in range(RING):
            landed(mid.at[0, q, y], s1_recv.at[0, q, step])
            landed(mid.at[1, q, z], s1_recv.at[1, q, step])
        local, far = second(q)
        for copy in far + local:
            copy.start()
        return local, far

    def sent(q):
        for step in (1, 2, 3):
            remote(*first_y(q, step)).wait_send()
            remote(*first_z(q, step, everything)).wait_send()

    second_0 = pass_on(0)
    for near, far in zip(tok_near, tok_far):
        near.wait_recv()
        far.start()

    def shuffle(cc, h, yy):
        to = 2 * c + h
        src, dst = ob.at[:, 0, yy, :, cc, 48 * h : 48 * h + 48], xs.at[x, :, yy]
        far = remote(src, dst, xs_send.at[cc, h], xs_recv.at[x], device(y, z, cc, to))
        near = pltpu.make_async_copy(src, dst, xs_recv.at[x])
        return jnp.logical_and(cc == c, to == x), near, far

    sent(0)

    @pl.loop(0, 4)
    def _(n):
        slot = n % 2
        load(down_w, n, slot, 0).wait()

        @pl.when(n < 3)
        def _():
            load(down_w, n + 1, 1 - slot, 0).start()

        for e in (0, 1):
            encode(slot, 0, e, (e, 0, n))
        for cc in (0, 1):
            for h in (0, 1):
                own, near, far = shuffle(cc, h, n)
                pl.when(own)(near.start)
                pl.when(jnp.logical_not(own))(far.start)

    second_1 = pass_on(1)

    def arrived(copies):
        local, far = copies
        for copy in local:
            copy.wait()
        for copy in far:
            copy.wait_recv()

    turned = jnp.transpose(block_tokens[...])
    for n in range(SLOTS):
        picks[n] = jnp.broadcast_to(turned[:, n : n + 1], (BLOCK, LANES))

    def show(n):
        return pltpu.make_async_copy(raw.at[ring(x, n)], shown.at[n % 2], shown_sem.at[n % 2])

    for copy in tok_far:
        copy.wait_recv()
    own_tokens = pltpu.make_async_copy(tokens, shown.at[0], shown_sem.at[0])
    own_tokens.start()
    for n in range(RING):
        if n < RING - 1:
            show(n + 1).start()
        (show(n) if n else own_tokens).wait()

        @pl.loop(0, 4)
        def _(i):
            rows = pl.ds(pl.multiple_of(i * 256, 256), 256)
            tok[ring(x, n), rows, :] = lax.dot_general(
                shown[n % 2, :, rows], place[...], (((0,), (0,)), ((), ())), preferred_element_type=F32
            ).astype(BF16)

    def products(e, half):
        @pl.loop(2 * half, 2 * half + 2)
        def _(n):
            rows = pl.ds(pl.multiple_of(n * 256, 256), 256)
            made = []
            for ab in (0, 1):
                total = None
                for s in range(RING):
                    weight = inbox[4 * ab + s, :, :, e].reshape(WIDE, COLS)
                    part = jnp.dot(tok[s, rows, :], weight, preferred_element_type=F32)
                    total = part if total is None else total + part
                made.append(total)
            gate, up = made
            hid_0[e, rows, :] = ((up + 1.0) * gate * jax.nn.sigmoid(1.702 * gate)).astype(BF16)

    hid_near, hid_far = [], []
    low, high = slice(0, 512), slice(512, TOK)
    for e in (0, 1):
        hid_near.append([
            remote(hid_0.at[e, low], hid_1.at[e, low], hid_send.at[e, 0], hid_recv.at[e, 0], right),
            remote(hid_0.at[e, high], hid_2.at[e, high], hid_send.at[e, 1], hid_recv.at[e, 1], left),
            remote(hid_0.at[e, high], hid_1.at[e, high], hid_send.at[e, 2], hid_recv.at[e, 2], right),
            remote(hid_0.at[e, low], hid_2.at[e, low], hid_send.at[e, 3], hid_recv.at[e, 3], left),
        ])
        hid_far.append([
            remote(hid_1.at[e, low], hid_3.at[e, low], hid_send.at[e, 4], hid_recv.at[e, 4], right),
            remote(hid_2.at[e, high], hid_3.at[e, high], hid_send.at[e, 5], hid_recv.at[e, 5], left),
        ])

    def gather_hidden(e):
        products(e, 0)
        hid_near[e][0].start()
        products(e, 1)
        for copy in hid_near[e][1:]:
            copy.start()

    def hid_forward(e, side):
        hid_near[e][side].wait_recv()
        hid_far[e][side].start()

    arrived(second_0)
    gather_hidden(0)

    for n in range(RING):
        landed(xs.at[n], xs_recv.at[n])

    def down_first(r):
        local, far = [], []
        for step in (2, 1, 3, 0):
            yy, zz = ring(y, step), ring(z, step)
            rows = pl.ds(r * TILE, TILE)
            a = (xs.at[:, 0, yy, :, rows], midd.at[0, r, :, y])
            b = (xs.at[:, 1, :, zz, rows], midd.at[1, r, :, z])
            if step == 0:
                local += [pltpu.make_async_copy(*pair, d1_recv.at[ab, r, 0]) for ab, pair in enumerate((a, b))]
                continue
            for ab, pair, target in ((0, a, device(yy, z, c, x)), (1, b, device(y, zz, c, x))):
                far.append(remote(*pair, d1_send.at[ab, r, step], d1_recv.at[ab, r, step], target))
        return local, far

    def down_second(r):
        local, far = [], []
        for step in (2, 1, 3, 0):
            yy, zz = ring(y, step), ring(z, step)
            a = (midd.at[0, r, :, :, zz], in_d[r].at[0, :, :, z])
            b = (midd.at[1, r, :, :, yy], in_d[r].at[1, :, y])
            if step == 0:
                local += [pltpu.make_async_copy(*pair, d2_recv.at[ab, r, 0]) for ab, pair in enumerate((a, b))]
                continue
            for ab, pair, target in ((0, a, device(y, zz, c, x)), (1, b, device(yy, z, c, x))):
                far.append(remote(*pair, d2_send.at[ab, r, step], d2_recv.at[ab, r, step], target))
        return local, far

    def start(copies):
        for copy in copies[1] + copies[0]:
            copy.start()

    down_1 = [down_first(r) for r in range(CHUNKS)]
    down_2 = [down_second(r) for r in range(CHUNKS)]
    for copies in down_1:
        start(copies)

    arrived(second_1)
    gather_hidden(1)

    load_order = pltpu.make_async_copy(order, inbox, order_sem)
    load_order.start()

    arrived(down_1[0])
    start(down_2[0])
    hid_forward(0, 0)
    hid_forward(0, 1)
    hid_forward(1, 0)
    arrived(down_1[1])
    start(down_2[1])
    hid_forward(1, 1)
    arrived(down_1[2])
    start(down_2[2])
    for copy in hid_near[0][2:] + hid_near[1][2:]:
        copy.wait_recv()

    results = []

    first, total = counts[0], counts[0] + counts[1]
    lanes = lax.broadcasted_iota(jnp.int32, (BLOCK, LANES), 1)

    def kept(h, step, n):
        return step, slice(n * BLOCK, (n + 1) * BLOCK), slice(h * COLS, (h + 1) * COLS)

    def pick(h, step, shards):
        slot = 2 * ring(x, step) + h
        row = jnp.where(slot < total, picks[slot], -1)
        chosen = jnp.concatenate([(row - n * LANES == lanes).astype(F32) for n in range(TOK // LANES)], axis=1).astype(BF16)
        which = (slot >= first).astype(jnp.int32)
        for n in shards:
            tok[kept(h, step, n)] = jnp.dot(chosen, hid[n][which], preferred_element_type=F32).astype(BF16)

    def project(h, r, step):
        to = ring(x, step)
        which = (2 * to + h >= first).astype(jnp.int32)
        made = None
        for n, away in enumerate((0, 3, 1, 2)):
            part = lax.dot_general(
                tok[kept(h, step, n)],
                in_d[r][which, ring(x, away)].reshape(BLOCK, COLS),
                (((1,), (1,)), ((), ())),
                preferred_element_type=F32,
            )
            made = part if made is None else made + part
        if step == 0:
            fin[x, h, r] = made.astype(BF16)
            return
        ob_out[step - 1, h, r] = made.astype(BF16)
        copy = remote(
            ob_out.at[step - 1, h, r], fin.at[x, h, r], out_send.at[h, r, step - 1], out_recv.at[h, r, step - 1],
            device(y, z, c, to),
        )
        copy.start()
        results.append((h, r, copy))

    for step in (2, 1, 3, 0):
        pick(0, step, (0, 1, 2))
    arrived(down_2[0])
    for copy in hid_far[0] + hid_far[1]:
        copy.wait_recv()
    for step in (2, 1, 3, 0):
        pick(0, step, (3,))
        project(0, 0, step)
    arrived(down_2[1])
    for step in (2, 1, 3, 0):
        project(0, 1, step)
    for step in (2, 1, 3, 0):
        pick(1, step, (0, 1, 2, 3))
        project(1, 0, step)
        project(1, 1, step)
    arrived(down_2[2])
    for h in (0, 1):
        for step in (2, 1, 3, 0):
            project(h, 2, step)

    load_order.wait()

    def ordered(h, half, matrix):
        result = None
        table = inbox[matrix].reshape(RING * OUTB, OUTB)
        for n in range(RING):
            got = [fin[n, h, r, :, half * LANES : (half + 1) * LANES] for r in range(CHUNKS)]
            part = lax.dot_general(
                table[n * OUTB : (n + 1) * OUTB],
                jnp.concatenate(got, axis=1),
                (((1,), (1,)), ((), ())),
                preferred_element_type=F32,
            )
            result = part if result is None else result + part
        return result

    def keep(b, h):
        rows = pl.ds(pl.multiple_of(b * OUTB, OUTB), OUTB) if not isinstance(b, int) else pl.ds(b * OUTB, min(OUTB, D - b * OUTB))
        spot = (rows, slice(h * BLOCK, (h + 1) * BLOCK))
        return spot, pltpu.make_async_copy(made_out.at[spot], out.at[spot], made_sem.at[h, b])

    def store(b, h, value):
        spot, copy = keep(b, h)
        made_out[spot] = value.astype(BF16)
        copy.start()

    for h in (0, 1):
        for hh, _, copy in results:
            if hh == h:
                copy.wait_recv()

        @pl.loop(0, 3)
        def _(b):
            store(b, h, ordered(h, 0, b))

        store(3, h, ordered(h, 0, 3) + ordered(h, 1, 8))

        @pl.loop(4, 7)
        def _(b):
            store(b, h, ordered(h, 1, b))

        store(7, h, ordered(h, 1, 7)[: D - 7 * OUTB])

    sent(1)
    for cc in (0, 1):
        for h in (0, 1):
            own, _, far = shuffle(cc, h, everything)
            pl.when(jnp.logical_not(own))(far.wait_send)
    for copies in (second_0, second_1, *down_1, *down_2):
        for copy in copies[1]:
            copy.wait_send()
    for h in (0, 1):
        for b in range(8):
            keep(b, h)[1].wait()
    for copy in tok_near + tok_far + sum(hid_near + hid_far, []) + [copy for _, _, copy in results]:
        copy.wait_send()


def body(tokens, gate_weight, up_weight, down_weight, block_counts, block_tokens):
    vmem, hbm = pl.BlockSpec(memory_space=pltpu.VMEM), pl.BlockSpec(memory_space=pltpu.HBM)
    dma = pltpu.SemaphoreType.DMA
    made = pl.pallas_call(
        kernel,
        out_shape=(
            jax.ShapeDtypeStruct((D, 2 * BLOCK), BF16),
            jax.ShapeDtypeStruct((2, 2, RING, RING, 2, PAD, COLS), BF16),
            jax.ShapeDtypeStruct((RING, 2, RING, RING, 48, COLS), BF16),
            jax.ShapeDtypeStruct((2, CHUNKS, RING, RING, RING, TILE, COLS), BF16),
            jax.ShapeDtypeStruct((RING, FEAT, TOK), BF16),
        ),
        in_specs=[hbm, hbm, hbm, hbm, vmem, pl.BlockSpec(memory_space=pltpu.SMEM), vmem, vmem, vmem, hbm],
        out_specs=(hbm, hbm, hbm, hbm, hbm),
        scratch_shapes=[
            pltpu.VMEM((2, 2, RING, RING, 2, PAD, COLS), BF16),
            pltpu.VMEM((9, RING, 2, 2, PAD, COLS), BF16),
            pltpu.VMEM((RING, TOK, WIDE), BF16),
            pltpu.VMEM((2, 2, PAD, 16, COLS), BF16),
            *[pltpu.VMEM((2, RING, RING, RING, TILE, COLS), BF16) for _ in range(CHUNKS)],
            *[pltpu.VMEM((2, TOK, COLS), BF16) for _ in range(RING)],
            pltpu.VMEM((3, 2, CHUNKS, BLOCK, BLOCK), BF16),
            pltpu.VMEM((RING, 2, CHUNKS, BLOCK, BLOCK), BF16),
            pltpu.VMEM((SLOTS, BLOCK, LANES), jnp.int32),
            pltpu.VMEM((2, FEAT, TOK), BF16),
            pltpu.VMEM((D, 2 * BLOCK), BF16),
            dma((2, 2)),
            dma,
            dma((2,)),
            dma((2, 8)),
            dma((2, 2, RING)), dma((2, 2, RING)),
            dma((2, 2, RING, 2)), dma((2, 2, RING, 2)),
            dma((2, 2)), dma((RING,)),
            dma((2, CHUNKS, RING)), dma((2, CHUNKS, RING)),
            dma((2, CHUNKS, RING)), dma((2, CHUNKS, RING)),
            dma((RING,)), dma((RING,)),
            dma((2, 6)), dma((2, 6)),
            dma((2, CHUNKS, 3)), dma((2, CHUNKS, 3)),
        ],
        compiler_params=pltpu.CompilerParams(
            collective_id=0, has_side_effects=True, vmem_limit_bytes=60 * 2**20
        ),
    )(
        tokens.T,
        *[jnp.swapaxes(weight, 0, 1) for weight in (gate_weight, up_weight, down_weight)],
        block_tokens,
        block_counts,
        jnp.asarray(place_matrix(), BF16),
        jnp.asarray(group_matrix(), BF16),
        jnp.asarray(swap_matrix(), BF16),
        jnp.asarray(order_matrix(), BF16).reshape(9, RING, 2, 2, PAD, COLS),
    )
    return made[0].T


def solution(mesh):
    in_specs = (
        P("expert", "shard"),
        P(None, "expert", "shard"),
        P(None, "expert", "shard"),
        P(None, "expert", "shard"),
        P("expert"),
        P("expert", None),
    )
    out_specs = P(("expert", "shard"), None)
    return jax.shard_map(body, mesh=mesh, in_specs=in_specs, out_specs=out_specs, check_vma=False)
```

```python
import functools

import jax
import jax.numpy as jnp
import numpy as np
from jax import lax
from jax.experimental import pallas as pl
from jax.experimental.pallas import tpu as pltpu
from jax.sharding import PartitionSpec as P

GROUP = 32
LANES = 128
BF16 = jnp.bfloat16
F32 = jnp.float32
MESH = pl.DeviceIdType.MESH

RING = 4
D = 2880
ROWS = 90
PAD = 96
FEAT = 720
WIDE = 8 * PAD
COLS = 384
TOK = 1024
BLOCK = 256
SLOTS = 8
TILE = 16
CHUNKS = 3
OUTB = 384


def place_matrix():
    m = np.zeros((FEAT, WIDE), np.float32)
    for k in range(FEAT):
        m[k, k // ROWS * PAD + k % ROWS] = 1
    return m


def group_matrix():
    lane = np.arange(LANES) // GROUP
    return (lane[:, None] == lane[None, :]).astype(np.float32)


def swap_matrix():
    m = np.zeros((2, LANES, BLOCK), np.float32)
    for e in range(2):
        for k in range(LANES):
            m[e, k, k % 16 * 16 + k // 16 * 2 + e] = 1
    return m


def order_matrix():
    m = np.zeros((9, RING, OUTB, OUTB), np.float32)
    for d in range(D):
        pair, rest = divmod(d, 2 * ROWS)
        core, row = divmod(rest, ROWS)
        part, row = divmod(row, 48)
        chunk, row = divmod(row, TILE)
        half, pair = divmod(pair, 8)
        block, col = divmod(d, OUTB)
        if block == 3 and half == 1:
            block = 8
        m[block, 2 * core + part, col, chunk * LANES + pair * TILE + row] = 1
    return m


def power_floor(value):
    far = value * 8388609.0
    return far - (far - value)


def restore(weight, groups):
    power = power_floor(jnp.abs(weight) * 0.751953125)
    square = power * power
    sixth = (square * square) * (square * 2.0**60)
    total = jnp.dot(sixth.astype(BF16), groups, preferred_element_type=F32)
    top = power_floor(jnp.exp2((jnp.log2(total) - 60.0) * (1.0 / 6.0)) * 0.8)
    top = jnp.minimum(jnp.maximum(top, 2.0**-30), 2.0**8)
    magic = jnp.maximum(power, top * 0.25) * (1.5 * 2.0**22)
    rounded = (weight + magic) - magic
    limit = top * 1.5
    return jnp.minimum(jnp.maximum(rounded, -limit), limit).astype(BF16)


def kernel(
    tokens, gate_w, up_w, down_w, block_tokens, counts, place, groups, swap, order,
    out, mid, xs, midd, raw,
    ob, inbox, tok, stage, in_0, in_1, in_2, hid_0, hid_1, hid_2, hid_3, ob_out, fin, picks, shown, made_out,
    stage_sem, order_sem, shown_sem, made_sem, s1_send, s1_recv, s2_send, s2_recv, xs_send, xs_recv,
    d1_send, d1_recv, d2_send, d2_recv, tok_send, tok_recv, hid_send, hid_recv, out_send, out_recv,
):
    in_d = (in_0, in_1, in_2)
    hid = (hid_0, hid_1, hid_2, hid_3)
    me, x = lax.axis_index("expert"), lax.axis_index("shard")
    y, z, c = me // 8, (me // 2) % 4, me % 2

    def device(yy, zz, cc, xx):
        return ((yy * 4 + zz) * 2 + cc, xx)

    def ring(at, step):
        return (at + step) % RING

    def remote(src, dst, send, recv, target):
        return pltpu.make_async_remote_copy(
            src_ref=src, dst_ref=dst, send_sem=send, recv_sem=recv, device_id=target, device_id_type=MESH
        )

    def landed(ref, sem):
        pltpu.make_async_copy(ref, ref, sem).wait()

    barrier = pltpu.get_barrier_semaphore()
    peers = [device(y, z, 1 - c, x)]
    for step in (1, 2, 3):
        for cc in (c, 1 - c):
            peers += [device(ring(y, step), z, cc, x), device(y, ring(z, step), cc, x), device(y, z, cc, ring(x, step))]
    for peer in peers:
        pl.semaphore_signal(barrier, inc=1, device_id=peer, device_id_type=MESH)

    def load(weight, yy, slot, ab):
        return pltpu.make_async_copy(
            weight.at[:, pl.ds(yy * 16, 16)], stage.at[slot, ab, 0:ROWS], stage_sem.at[slot, ab]
        )

    load(gate_w, ring(y, 1), 0, 0).start()
    load(up_w, 0, 0, 1).start()
    stage[:, :, ROWS:PAD] = jnp.zeros((2, 2, PAD - ROWS, 16, COLS), BF16)
    turned = jnp.transpose(block_tokens[...])
    for n in range(SLOTS):
        picks[n] = jnp.broadcast_to(turned[:, n : n + 1], (BLOCK, LANES))

    pl.semaphore_wait(barrier, len(peers))

    right, left = device(y, z, c, ring(x, 1)), device(y, z, c, ring(x, 3))
    tok_near = [
        remote(tokens, raw.at[x], tok_send.at[0], tok_recv.at[0], right),
        remote(tokens, raw.at[x], tok_send.at[1], tok_recv.at[1], left),
    ]
    for copy in tok_near:
        copy.start()
    lower, upper = raw.at[ring(x, 3), 0:368], raw.at[ring(x, 1), 368:FEAT]
    tok_far = [
        remote(lower, lower, tok_send.at[2], tok_recv.at[2], right),
        remote(upper, upper, tok_send.at[3], tok_recv.at[3], left),
    ]

    def encode(slot, ab, e, to):
        @pl.loop(0, 6, unroll=3)
        def _(j):
            rows = pl.ds(pl.multiple_of(j * TILE, TILE), TILE)
            for lane in range(COLS // LANES):
                cols = slice(lane * LANES, (lane + 1) * LANES)
                block = stage[slot, ab, rows, :, cols].reshape(BLOCK, LANES)
                for n in (0, 1):
                    weight = jnp.dot(swap[e, n * 64 : n * 64 + 64, :], block, preferred_element_type=F32)
                    ob[*to, 2 * n : 2 * n + 2, :, rows, cols] = restore(weight, groups[...]).reshape(2, 2, TILE, LANES)

    def first_y(q, step):
        to = ring(y, step)
        return ob.at[0, q, to], mid.at[0, q, y], s1_send.at[0, q, step], s1_recv.at[0, q, step], device(to, z, c, x)

    def first_z(q, step, yy):
        to = ring(z, step)
        send, recv = s1_send.at[1, q, step], s1_recv.at[1, q, step]
        return ob.at[1, q, yy, to], mid.at[1, q, z, yy], send, recv, device(y, to, c, x)

    @pl.loop(0, 8)
    def _(n):
        slot, q, i = n % 2, n // 4, n % 4
        load(gate_w, ring(y, i + 1), slot, 0).wait()
        load(up_w, i, slot, 1).wait()

        @pl.when(n < 7)
        def _():
            load(gate_w, ring(y, n + 2), 1 - slot, 0).start()
            load(up_w, (n + 1) % 4, 1 - slot, 1).start()

        encode(slot, 0, q, (0, q, ring(y, i + 1)))

        @pl.when(i == 3)
        def _():
            src, dst, _, recv, _ = first_y(q, 0)
            pltpu.make_async_copy(src, dst, recv).start()

        @pl.when(i != 3)
        def _():
            remote(*first_y(q, i + 1)).start()

        encode(slot, 1, q, (1, q, i))
        for step in (2, 1, 3):
            remote(*first_z(q, step, i)).start()
        src, dst, _, recv, _ = first_z(q, 0, i)
        pltpu.make_async_copy(src, dst, recv).start()

    load(down_w, 0, 0, 0).start()
    everything = slice(None)

    def second(q):
        local, far = [], []
        for step in (2, 1, 3, 0):
            for dc in (0, 1):
                cc = (c + dc) % 2
                zz, yy = ring(z, step), ring(y, step)
                a = (mid.at[0, q, :, zz, cc], inbox.at[0:4, z, c, q])
                b = (mid.at[1, q, :, yy, cc], inbox.at[4 + y, :, c, q])
                if step == 0 and dc == 0:
                    local += [pltpu.make_async_copy(*pair, s2_recv.at[ab, q, 0, 0]) for ab, pair in enumerate((a, b))]
                    continue
                for ab, pair, target in ((0, a, device(y, zz, cc, x)), (1, b, device(yy, z, cc, x))):
                    far.append(remote(*pair, s2_send.at[ab, q, step, dc], s2_recv.at[ab, q, step, dc], target))
        return local, far

    def pass_on(q):
        for step in range(RING):
            landed(mid.at[0, q, y], s1_recv.at[0, q, step])
            landed(mid.at[1, q, z], s1_recv.at[1, q, step])
        local, far = second(q)
        for copy in far + local:
            copy.start()
        return local, far

    def sent(q):
        for step in (1, 2, 3):
            remote(*first_y(q, step)).wait_send()
            remote(*first_z(q, step, everything)).wait_send()

    second_0 = pass_on(0)
    for near, far in zip(tok_near, tok_far):
        near.wait_recv()
        far.start()

    def shuffle(cc, h, yy):
        to = 2 * c + h
        src, dst = ob.at[:, 0, yy, :, cc, 48 * h : 48 * h + 48], xs.at[x, :, yy]
        far = remote(src, dst, xs_send.at[cc, h], xs_recv.at[x], device(y, z, cc, to))
        near = pltpu.make_async_copy(src, dst, xs_recv.at[x])
        return jnp.logical_and(cc == c, to == x), near, far

    sent(0)

    @pl.loop(0, 4)
    def _(n):
        slot = n % 2
        load(down_w, n, slot, 0).wait()

        @pl.when(n < 3)
        def _():
            load(down_w, n + 1, 1 - slot, 0).start()

        for e in (0, 1):
            encode(slot, 0, e, (e, 0, n))
        for cc in (0, 1):
            for h in (0, 1):
                own, near, far = shuffle(cc, h, n)
                pl.when(own)(near.start)
                pl.when(jnp.logical_not(own))(far.start)

    second_1 = pass_on(1)

    def arrived(copies):
        local, far = copies
        for copy in local:
            copy.wait()
        for copy in far:
            copy.wait_recv()

    def show(n):
        return pltpu.make_async_copy(raw.at[ring(x, n)], shown.at[n % 2], shown_sem.at[n % 2])

    for copy in tok_far:
        copy.wait_recv()
    own_tokens = pltpu.make_async_copy(tokens, shown.at[0], shown_sem.at[0])
    own_tokens.start()
    for n in range(RING):
        if n < RING - 1:
            show(n + 1).start()
        (show(n) if n else own_tokens).wait()

        @pl.loop(0, 4)
        def _(i):
            rows = pl.ds(pl.multiple_of(i * 256, 256), 256)
            tok[ring(x, n), rows, :] = lax.dot_general(
                shown[n % 2, :, rows], place[...], (((0,), (0,)), ((), ())), preferred_element_type=F32
            ).astype(BF16)

    def products(e):
        @pl.loop(0, 4)
        def _(n):
            rows = pl.ds(pl.multiple_of(n * 256, 256), 256)
            made = []
            for ab in (0, 1):
                total = None
                for s in range(RING):
                    weight = inbox[4 * ab + s, :, :, e].reshape(WIDE, COLS)
                    part = jnp.dot(tok[s, rows, :], weight, preferred_element_type=F32)
                    total = part if total is None else total + part
                made.append(total)
            gate, up = made
            hid_0[e, rows, :] = ((up + 1.0) * gate * jax.nn.sigmoid(1.702 * gate)).astype(BF16)

    hid_near, hid_far = [], []
    low, high = slice(0, 512), slice(512, TOK)
    for e in (0, 1):
        hid_near.append([
            remote(hid_0.at[e], hid_1.at[e], hid_send.at[e, 0], hid_recv.at[e, 0], right),
            remote(hid_0.at[e], hid_2.at[e], hid_send.at[e, 1], hid_recv.at[e, 1], left),
        ])
        hid_far.append([
            remote(hid_1.at[e, low], hid_3.at[e, low], hid_send.at[e, 2], hid_recv.at[e, 2], right),
            remote(hid_2.at[e, high], hid_3.at[e, high], hid_send.at[e, 3], hid_recv.at[e, 3], left),
        ])

    arrived(second_0)
    products(0)
    for copy in hid_near[0]:
        copy.start()

    for n in range(RING):
        landed(xs.at[n], xs_recv.at[n])

    def down_first(r):
        local, far = [], []
        for step in (2, 1, 3, 0):
            yy, zz = ring(y, step), ring(z, step)
            rows = pl.ds(r * TILE, TILE)
            a = (xs.at[:, 0, yy, :, rows], midd.at[0, r, :, y])
            b = (xs.at[:, 1, :, zz, rows], midd.at[1, r, :, z])
            if step == 0:
                local += [pltpu.make_async_copy(*pair, d1_recv.at[ab, r, 0]) for ab, pair in enumerate((a, b))]
                continue
            for ab, pair, target in ((0, a, device(yy, z, c, x)), (1, b, device(y, zz, c, x))):
                far.append(remote(*pair, d1_send.at[ab, r, step], d1_recv.at[ab, r, step], target))
        return local, far

    def down_second(r):
        local, far = [], []
        for step in (2, 1, 3, 0):
            yy, zz = ring(y, step), ring(z, step)
            a = (midd.at[0, r, :, :, zz], in_d[r].at[0, :, :, z])
            b = (midd.at[1, r, :, :, yy], in_d[r].at[1, :, y])
            if step == 0:
                local += [pltpu.make_async_copy(*pair, d2_recv.at[ab, r, 0]) for ab, pair in enumerate((a, b))]
                continue
            for ab, pair, target in ((0, a, device(y, zz, c, x)), (1, b, device(yy, z, c, x))):
                far.append(remote(*pair, d2_send.at[ab, r, step], d2_recv.at[ab, r, step], target))
        return local, far

    def start(copies):
        for copy in copies[1] + copies[0]:
            copy.start()

    down_1 = [down_first(r) for r in range(CHUNKS)]
    down_2 = [down_second(r) for r in range(CHUNKS)]
    for copies in down_1:
        start(copies)

    arrived(second_1)
    products(1)
    for copy in hid_near[1]:
        copy.start()

    load_order = pltpu.make_async_copy(order, inbox, order_sem)
    load_order.start()

    def hid_forward(h):
        for near, far in zip(hid_near[h], hid_far[h]):
            near.wait_recv()
            far.start()

    arrived(down_1[0])
    start(down_2[0])
    hid_forward(0)
    arrived(down_1[1])
    start(down_2[1])
    hid_forward(1)
    arrived(down_1[2])
    start(down_2[2])

    results = []

    first, total = counts[0], counts[0] + counts[1]
    lanes = lax.broadcasted_iota(jnp.int32, (BLOCK, LANES), 1)

    def kept(h, step, n):
        return step, slice(n * BLOCK, (n + 1) * BLOCK), slice(h * COLS, (h + 1) * COLS)

    def pick(h, step, shards):
        slot = 2 * ring(x, step) + h
        row = jnp.where(slot < total, picks[slot], -1)
        chosen = jnp.concatenate([(row - n * LANES == lanes).astype(F32) for n in range(TOK // LANES)], axis=1).astype(BF16)
        which = (slot >= first).astype(jnp.int32)
        for n in shards:
            tok[kept(h, step, n)] = jnp.dot(chosen, hid[n][which], preferred_element_type=F32).astype(BF16)

    def project(h, r, step):
        to = ring(x, step)
        which = (2 * to + h >= first).astype(jnp.int32)
        made = None
        for n, away in enumerate((0, 3, 1, 2)):
            part = lax.dot_general(
                tok[kept(h, step, n)],
                in_d[r][which, ring(x, away)].reshape(BLOCK, COLS),
                (((1,), (1,)), ((), ())),
                preferred_element_type=F32,
            )
            made = part if made is None else made + part
        if step == 0:
            fin[x, h, r] = made.astype(BF16)
            return
        ob_out[step - 1, h, r] = made.astype(BF16)
        copy = remote(
            ob_out.at[step - 1, h, r], fin.at[x, h, r], out_send.at[h, r, step - 1], out_recv.at[h, r, step - 1],
            device(y, z, c, to),
        )
        copy.start()
        results.append((h, r, copy))

    for step in (2, 1, 3, 0):
        pick(0, step, (0, 1, 2))
    arrived(down_2[0])
    for copy in hid_far[0] + hid_far[1]:
        copy.wait_recv()
    for step in (2, 1, 3, 0):
        pick(0, step, (3,))
        project(0, 0, step)
    arrived(down_2[1])
    for step in (2, 1, 3, 0):
        project(0, 1, step)
    for step in (2, 1, 3, 0):
        pick(1, step, (0, 1, 2, 3))
        project(1, 0, step)
        project(1, 1, step)
    arrived(down_2[2])
    for h in (0, 1):
        for step in (2, 1, 3, 0):
            project(h, 2, step)

    load_order.wait()

    def ordered(h, half, matrix, last):
        table = inbox[matrix].reshape(RING * OUTB, OUTB)

        def pieces(n, r):
            left = table[n * OUTB : (n + 1) * OUTB, r * LANES : (r + 1) * LANES]
            return left, fin[n, h, r, :, half * LANES : (half + 1) * LANES]

        result = None
        for n in range(0, RING, 2):
            for pair in [[(n, 2), (n + 1, 2)]] if last else [[(n, 0), (n, 1)], [(n + 1, 0), (n + 1, 1)]]:
                left, right = zip(*[pieces(*at) for at in pair])
                part = lax.dot_general(
                    jnp.concatenate(left, axis=1),
                    jnp.concatenate(right, axis=1),
                    (((1,), (1,)), ((), ())),
                    preferred_element_type=F32,
                )
                result = part if result is None else result + part
        return result

    def keep(b, h):
        rows = pl.ds(pl.multiple_of(b * OUTB, OUTB), OUTB) if not isinstance(b, int) else pl.ds(b * OUTB, min(OUTB, D - b * OUTB))
        spot = (rows, slice(h * BLOCK, (h + 1) * BLOCK))
        return spot, pltpu.make_async_copy(made_out.at[spot], out.at[spot], made_sem.at[h, b])

    def store(b, h, value, last):
        spot, copy = keep(b, h)
        if last:
            made_out[spot] = (made_out[spot].astype(F32) + value).astype(BF16)
            copy.start()
        else:
            made_out[spot] = value.astype(BF16)

    for last in (False, True):
        for h in (0, 1):
            for hh, r, copy in results:
                if hh == h and (r == 2) == last:
                    copy.wait_recv()

            @pl.loop(0, 3)
            def _(b):
                store(b, h, ordered(h, 0, b, last), last)

            store(3, h, ordered(h, 0, 3, last) + ordered(h, 1, 8, last), last)

            @pl.loop(4, 7)
            def _(b):
                store(b, h, ordered(h, 1, b, last), last)

            store(7, h, ordered(h, 1, 7, last)[: D - 7 * OUTB], last)

    sent(1)
    for cc in (0, 1):
        for h in (0, 1):
            own, _, far = shuffle(cc, h, everything)
            pl.when(jnp.logical_not(own))(far.wait_send)
    for copies in (second_0, second_1, *down_1, *down_2):
        for copy in copies[1]:
            copy.wait_send()
    for h in (0, 1):
        for b in range(8):
            keep(b, h)[1].wait()
    for copy in tok_near + tok_far + sum(hid_near + hid_far, []) + [copy for _, _, copy in results]:
        copy.wait_send()


def body(tokens, gate_weight, up_weight, down_weight, block_counts, block_tokens):
    vmem, hbm = pl.BlockSpec(memory_space=pltpu.VMEM), pl.BlockSpec(memory_space=pltpu.HBM)
    dma = pltpu.SemaphoreType.DMA
    made = pl.pallas_call(
        kernel,
        out_shape=(
            jax.ShapeDtypeStruct((D, 2 * BLOCK), BF16),
            jax.ShapeDtypeStruct((2, 2, RING, RING, 2, PAD, COLS), BF16),
            jax.ShapeDtypeStruct((RING, 2, RING, RING, 48, COLS), BF16),
            jax.ShapeDtypeStruct((2, CHUNKS, RING, RING, RING, TILE, COLS), BF16),
            jax.ShapeDtypeStruct((RING, FEAT, TOK), BF16),
        ),
        in_specs=[hbm, hbm, hbm, hbm, vmem, pl.BlockSpec(memory_space=pltpu.SMEM), vmem, vmem, vmem, hbm],
        out_specs=(hbm, hbm, hbm, hbm, hbm),
        scratch_shapes=[
            pltpu.VMEM((2, 2, RING, RING, 2, PAD, COLS), BF16),
            pltpu.VMEM((9, RING, 2, 2, PAD, COLS), BF16),
            pltpu.VMEM((RING, TOK, WIDE), BF16),
            pltpu.VMEM((2, 2, PAD, 16, COLS), BF16),
            *[pltpu.VMEM((2, RING, RING, RING, TILE, COLS), BF16) for _ in range(CHUNKS)],
            *[pltpu.VMEM((2, TOK, COLS), BF16) for _ in range(RING)],
            pltpu.VMEM((3, 2, CHUNKS, BLOCK, BLOCK), BF16),
            pltpu.VMEM((RING, 2, CHUNKS, BLOCK, BLOCK), BF16),
            pltpu.VMEM((SLOTS, BLOCK, LANES), jnp.int32),
            pltpu.VMEM((2, FEAT, TOK), BF16),
            pltpu.VMEM((D, 2 * BLOCK), BF16),
            dma((2, 2)),
            dma,
            dma((2,)),
            dma((2, 8)),
            dma((2, 2, RING)), dma((2, 2, RING)),
            dma((2, 2, RING, 2)), dma((2, 2, RING, 2)),
            dma((2, 2)), dma((RING,)),
            dma((2, CHUNKS, RING)), dma((2, CHUNKS, RING)),
            dma((2, CHUNKS, RING)), dma((2, CHUNKS, RING)),
            dma((RING,)), dma((RING,)),
            dma((2, RING)), dma((2, RING)),
            dma((2, CHUNKS, 3)), dma((2, CHUNKS, 3)),
        ],
        compiler_params=pltpu.CompilerParams(
            collective_id=0, has_side_effects=True, vmem_limit_bytes=60 * 2**20
        ),
    )(
        tokens.T,
        *[jnp.swapaxes(weight, 0, 1) for weight in (gate_weight, up_weight, down_weight)],
        block_tokens,
        block_counts,
        jnp.asarray(place_matrix(), BF16),
        jnp.asarray(group_matrix(), BF16),
        jnp.asarray(swap_matrix(), BF16),
        jnp.asarray(order_matrix(), BF16).reshape(9, RING, 2, 2, PAD, COLS),
    )
    return made[0].T


def solution(mesh):
    in_specs = (
        P("expert", "shard"),
        P(None, "expert", "shard"),
        P(None, "expert", "shard"),
        P(None, "expert", "shard"),
        P("expert"),
        P("expert", None),
    )
    out_specs = P(("expert", "shard"), None)
    return jax.shard_map(body, mesh=mesh, in_specs=in_specs, out_specs=out_specs, check_vma=False)
```

```python
import functools

import jax
import jax.numpy as jnp
import numpy as np
from jax import lax
from jax.experimental import pallas as pl
from jax.experimental.pallas import tpu as pltpu
from jax.sharding import PartitionSpec as P

GROUP = 32
LANES = 128
BF16 = jnp.bfloat16
F32 = jnp.float32
MESH = pl.DeviceIdType.MESH

RING = 4
D = 2880
ROWS = 90
PAD = 96
FEAT = 720
WIDE = 8 * PAD
COLS = 384
TOK = 1024
BLOCK = 256
SLOTS = 8
TILE = 16
CHUNKS = 3
OUTB = 384


def place_matrix():
    m = np.zeros((FEAT, WIDE), np.float32)
    for k in range(FEAT):
        m[k, k // ROWS * PAD + k % ROWS] = 1
    return m


def group_matrix():
    lane = np.arange(LANES) // GROUP
    return (lane[:, None] == lane[None, :]).astype(np.float32)


def swap_matrix():
    m = np.zeros((2, LANES, BLOCK), np.float32)
    for e in range(2):
        for k in range(LANES):
            m[e, k, k % 16 * 16 + k // 16 * 2 + e] = 1
    return m


def order_matrix():
    m = np.zeros((9, RING, OUTB, OUTB), np.float32)
    for d in range(D):
        pair, rest = divmod(d, 2 * ROWS)
        core, row = divmod(rest, ROWS)
        part, row = divmod(row, 48)
        chunk, row = divmod(row, TILE)
        half, pair = divmod(pair, 8)
        block, col = divmod(d, OUTB)
        if block == 3 and half == 1:
            block = 8
        m[block, 2 * core + part, col, chunk * LANES + pair * TILE + row] = 1
    return m


def power_floor(value):
    far = value * 8388609.0
    return far - (far - value)


def restore(weight, groups):
    power = power_floor(jnp.abs(weight) * 0.751953125)
    square = power * power
    sixth = (square * square) * (square * 2.0**60)
    total = jnp.dot(sixth.astype(BF16), groups, preferred_element_type=F32)
    top = power_floor(jnp.exp2((jnp.log2(total) - 60.0) * (1.0 / 6.0)) * 0.8)
    top = jnp.minimum(jnp.maximum(top, 2.0**-30), 2.0**8)
    magic = jnp.maximum(power, top * 0.25) * (1.5 * 2.0**22)
    rounded = (weight + magic) - magic
    limit = top * 1.5
    return jnp.minimum(jnp.maximum(rounded, -limit), limit).astype(BF16)


def kernel(
    tokens, gate_w, up_w, down_w, block_tokens, counts, place, groups, swap, order,
    out, mid, xs, midd, raw,
    ob, inbox, tok, stage, in_0, in_1, in_2, hid_0, hid_1, hid_2, hid_3, ob_out, fin, picks, shown, made_out,
    stage_sem, order_sem, shown_sem, made_sem, s1_send, s1_recv, s2_send, s2_recv, xs_send, xs_recv,
    d1_send, d1_recv, d2_send, d2_recv, tok_send, tok_recv, hid_send, hid_recv, out_send, out_recv,
):
    in_d = (in_0, in_1, in_2)
    hid = (hid_0, hid_1, hid_2, hid_3)
    me, x = lax.axis_index("expert"), lax.axis_index("shard")
    y, z, c = me // 8, (me // 2) % 4, me % 2

    def device(yy, zz, cc, xx):
        return ((yy * 4 + zz) * 2 + cc, xx)

    def ring(at, step):
        return (at + step) % RING

    def remote(src, dst, send, recv, target):
        return pltpu.make_async_remote_copy(
            src_ref=src, dst_ref=dst, send_sem=send, recv_sem=recv, device_id=target, device_id_type=MESH
        )

    def landed(ref, sem):
        pltpu.make_async_copy(ref, ref, sem).wait()

    barrier = pltpu.get_barrier_semaphore()
    peers = [device(y, z, 1 - c, x)]
    for step in (1, 2, 3):
        for cc in (c, 1 - c):
            peers += [device(ring(y, step), z, cc, x), device(y, ring(z, step), cc, x), device(y, z, cc, ring(x, step))]
    for peer in peers:
        pl.semaphore_signal(barrier, inc=1, device_id=peer, device_id_type=MESH)

    def load(weight, yy, slot, ab):
        return pltpu.make_async_copy(
            weight.at[:, pl.ds(yy * 16, 16)], stage.at[slot, ab, 0:ROWS], stage_sem.at[slot, ab]
        )

    load(gate_w, ring(y, 1), 0, 0).start()
    load(up_w, 0, 0, 1).start()
    stage[:, :, ROWS:PAD] = jnp.zeros((2, 2, PAD - ROWS, 16, COLS), BF16)
    turned = jnp.transpose(block_tokens[...])
    for n in range(SLOTS):
        picks[n] = jnp.broadcast_to(turned[:, n : n + 1], (BLOCK, LANES))

    pl.semaphore_wait(barrier, len(peers))

    right, left = device(y, z, c, ring(x, 1)), device(y, z, c, ring(x, 3))
    tok_near = [
        remote(tokens, raw.at[x], tok_send.at[0], tok_recv.at[0], right),
        remote(tokens, raw.at[x], tok_send.at[1], tok_recv.at[1], left),
    ]
    for copy in tok_near:
        copy.start()
    lower, upper = raw.at[ring(x, 3), 0:368], raw.at[ring(x, 1), 368:FEAT]
    tok_far = [
        remote(lower, lower, tok_send.at[2], tok_recv.at[2], right),
        remote(upper, upper, tok_send.at[3], tok_recv.at[3], left),
    ]

    def encode(slot, ab, e, to):
        @pl.loop(0, 6, unroll=3)
        def _(j):
            rows = pl.ds(pl.multiple_of(j * TILE, TILE), TILE)
            for lane in range(COLS // LANES):
                cols = slice(lane * LANES, (lane + 1) * LANES)
                block = stage[slot, ab, rows, :, cols].reshape(BLOCK, LANES)
                for n in (0, 1):
                    weight = jnp.dot(swap[e, n * 64 : n * 64 + 64, :], block, preferred_element_type=F32)
                    ob[*to, 2 * n : 2 * n + 2, :, rows, cols] = restore(weight, groups[...]).reshape(2, 2, TILE, LANES)

    def first_y(q, step):
        to = ring(y, step)
        return ob.at[0, q, to], mid.at[0, q, y], s1_send.at[0, q, step], s1_recv.at[0, q, step], device(to, z, c, x)

    def first_z(q, step, yy):
        to = ring(z, step)
        send, recv = s1_send.at[1, q, step], s1_recv.at[1, q, step]
        return ob.at[1, q, yy, to], mid.at[1, q, z, yy], send, recv, device(y, to, c, x)

    @pl.loop(0, 8)
    def _(n):
        slot, q, i = n % 2, n // 4, n % 4
        load(gate_w, ring(y, i + 1), slot, 0).wait()
        load(up_w, i, slot, 1).wait()

        @pl.when(n < 7)
        def _():
            load(gate_w, ring(y, n + 2), 1 - slot, 0).start()
            load(up_w, (n + 1) % 4, 1 - slot, 1).start()

        encode(slot, 0, q, (0, q, ring(y, i + 1)))

        @pl.when(i == 3)
        def _():
            src, dst, _, recv, _ = first_y(q, 0)
            pltpu.make_async_copy(src, dst, recv).start()

        @pl.when(i != 3)
        def _():
            remote(*first_y(q, i + 1)).start()

        encode(slot, 1, q, (1, q, i))
        for step in (2, 1, 3):
            remote(*first_z(q, step, i)).start()
        src, dst, _, recv, _ = first_z(q, 0, i)
        pltpu.make_async_copy(src, dst, recv).start()

    load(down_w, 0, 0, 0).start()
    everything = slice(None)

    def second(q):
        local, far = [], []
        for step in (2, 1, 3, 0):
            for dc in (0, 1):
                cc = (c + dc) % 2
                zz, yy = ring(z, step), ring(y, step)
                a = (mid.at[0, q, :, zz, cc], inbox.at[0:4, z, c, q])
                b = (mid.at[1, q, :, yy, cc], inbox.at[4 + y, :, c, q])
                if step == 0 and dc == 0:
                    local += [pltpu.make_async_copy(*pair, s2_recv.at[ab, q, 0, 0]) for ab, pair in enumerate((a, b))]
                    continue
                for ab, pair, target in ((0, a, device(y, zz, cc, x)), (1, b, device(yy, z, cc, x))):
                    far.append(remote(*pair, s2_send.at[ab, q, step, dc], s2_recv.at[ab, q, step, dc], target))
        return local, far

    def pass_on(q):
        for step in range(RING):
            landed(mid.at[0, q, y], s1_recv.at[0, q, step])
            landed(mid.at[1, q, z], s1_recv.at[1, q, step])
        local, far = second(q)
        for copy in far + local:
            copy.start()
        return local, far

    def sent(q):
        for step in (1, 2, 3):
            remote(*first_y(q, step)).wait_send()
            remote(*first_z(q, step, everything)).wait_send()

    second_0 = pass_on(0)
    for near, far in zip(tok_near, tok_far):
        near.wait_recv()
        far.start()

    def shuffle(cc, h, yy):
        to = 2 * c + h
        src, dst = ob.at[:, 0, yy, :, cc, 48 * h : 48 * h + 48], xs.at[x, :, yy]
        far = remote(src, dst, xs_send.at[cc, h], xs_recv.at[x], device(y, z, cc, to))
        near = pltpu.make_async_copy(src, dst, xs_recv.at[x])
        return jnp.logical_and(cc == c, to == x), near, far

    sent(0)

    @pl.loop(0, 4)
    def _(n):
        slot = n % 2
        load(down_w, n, slot, 0).wait()

        @pl.when(n < 3)
        def _():
            load(down_w, n + 1, 1 - slot, 0).start()

        for e in (0, 1):
            encode(slot, 0, e, (e, 0, n))
        for cc in (0, 1):
            for h in (0, 1):
                own, near, far = shuffle(cc, h, n)
                pl.when(own)(near.start)
                pl.when(jnp.logical_not(own))(far.start)

    second_1 = pass_on(1)

    def arrived(copies):
        local, far = copies
        for copy in local:
            copy.wait()
        for copy in far:
            copy.wait_recv()

    def show(n):
        return pltpu.make_async_copy(raw.at[ring(x, n)], shown.at[n % 2], shown_sem.at[n % 2])

    for copy in tok_far:
        copy.wait_recv()
    own_tokens = pltpu.make_async_copy(tokens, shown.at[0], shown_sem.at[0])
    own_tokens.start()
    for n in range(RING):
        if n < RING - 1:
            show(n + 1).start()
        (show(n) if n else own_tokens).wait()

        @pl.loop(0, 4)
        def _(i):
            rows = pl.ds(pl.multiple_of(i * 256, 256), 256)
            tok[ring(x, n), rows, :] = lax.dot_general(
                shown[n % 2, :, rows], place[...], (((0,), (0,)), ((), ())), preferred_element_type=F32
            ).astype(BF16)

    def products(e):
        @pl.loop(0, 4)
        def _(n):
            rows = pl.ds(pl.multiple_of(n * 256, 256), 256)
            made = []
            for ab in (0, 1):
                total = None
                for s in range(RING):
                    weight = inbox[4 * ab + s, :, :, e].reshape(WIDE, COLS)
                    part = jnp.dot(tok[s, rows, :], weight, preferred_element_type=F32)
                    total = part if total is None else total + part
                made.append(total)
            gate, up = made
            hid_0[e, rows, :] = ((up + 1.0) * gate * jax.nn.sigmoid(1.702 * gate)).astype(BF16)

    hid_near, hid_far = [], []
    low, high = slice(0, 512), slice(512, TOK)
    for e in (0, 1):
        hid_near.append([
            remote(hid_0.at[e], hid_1.at[e], hid_send.at[e, 0], hid_recv.at[e, 0], right),
            remote(hid_0.at[e], hid_2.at[e], hid_send.at[e, 1], hid_recv.at[e, 1], left),
        ])
        hid_far.append([
            remote(hid_1.at[e, low], hid_3.at[e, low], hid_send.at[e, 2], hid_recv.at[e, 2], right),
            remote(hid_2.at[e, high], hid_3.at[e, high], hid_send.at[e, 3], hid_recv.at[e, 3], left),
        ])

    arrived(second_0)
    products(0)
    for copy in hid_near[0]:
        copy.start()

    for n in range(RING):
        landed(xs.at[n], xs_recv.at[n])

    def down_first(r):
        local, far = [], []
        for step in (2, 1, 3, 0):
            yy, zz = ring(y, step), ring(z, step)
            rows = pl.ds(r * TILE, TILE)
            a = (xs.at[:, 0, yy, :, rows], midd.at[0, r, :, y])
            b = (xs.at[:, 1, :, zz, rows], midd.at[1, r, :, z])
            if step == 0:
                local += [pltpu.make_async_copy(*pair, d1_recv.at[ab, r, 0]) for ab, pair in enumerate((a, b))]
                continue
            for ab, pair, target in ((0, a, device(yy, z, c, x)), (1, b, device(y, zz, c, x))):
                far.append(remote(*pair, d1_send.at[ab, r, step], d1_recv.at[ab, r, step], target))
        return local, far

    def down_second(r):
        local, far = [], []
        for step in (2, 1, 3, 0):
            yy, zz = ring(y, step), ring(z, step)
            a = (midd.at[0, r, :, :, zz], in_d[r].at[0, :, :, z])
            b = (midd.at[1, r, :, :, yy], in_d[r].at[1, :, y])
            if step == 0:
                local += [pltpu.make_async_copy(*pair, d2_recv.at[ab, r, 0]) for ab, pair in enumerate((a, b))]
                continue
            for ab, pair, target in ((0, a, device(y, zz, c, x)), (1, b, device(yy, z, c, x))):
                far.append(remote(*pair, d2_send.at[ab, r, step], d2_recv.at[ab, r, step], target))
        return local, far

    def start(copies):
        for copy in copies[1] + copies[0]:
            copy.start()

    down_1 = [down_first(r) for r in range(CHUNKS)]
    down_2 = [down_second(r) for r in range(CHUNKS)]
    for copies in down_1:
        start(copies)

    arrived(second_1)
    products(1)
    for copy in hid_near[1]:
        copy.start()

    load_order = pltpu.make_async_copy(order, inbox, order_sem)
    load_order.start()

    def hid_forward(h):
        for near, far in zip(hid_near[h], hid_far[h]):
            near.wait_recv()
            far.start()

    arrived(down_1[0])
    start(down_2[0])
    hid_forward(0)
    arrived(down_1[1])
    start(down_2[1])
    hid_forward(1)
    arrived(down_1[2])
    start(down_2[2])

    results = []

    first, total = counts[0], counts[0] + counts[1]
    lanes = lax.broadcasted_iota(jnp.int32, (BLOCK, LANES), 1)

    def kept(h, step, n):
        return step, slice(n * BLOCK, (n + 1) * BLOCK), slice(h * COLS, (h + 1) * COLS)

    def pick(h, step, shards):
        slot = 2 * ring(x, step) + h
        row = jnp.where(slot < total, picks[slot], -1)
        chosen = jnp.concatenate([(row - n * LANES == lanes).astype(F32) for n in range(TOK // LANES)], axis=1).astype(BF16)
        which = (slot >= first).astype(jnp.int32)
        for n in shards:
            tok[kept(h, step, n)] = jnp.dot(chosen, hid[n][which], preferred_element_type=F32).astype(BF16)

    def project(h, r, step):
        to = ring(x, step)
        which = (2 * to + h >= first).astype(jnp.int32)
        made = None
        for n, away in enumerate((0, 3, 1, 2)):
            part = lax.dot_general(
                tok[kept(h, step, n)],
                in_d[r][which, ring(x, away)].reshape(BLOCK, COLS),
                (((1,), (1,)), ((), ())),
                preferred_element_type=F32,
            )
            made = part if made is None else made + part
        if step == 0:
            fin[x, h, r] = made.astype(BF16)
            return
        ob_out[step - 1, h, r] = made.astype(BF16)
        copy = remote(
            ob_out.at[step - 1, h, r], fin.at[x, h, r], out_send.at[h, r, step - 1], out_recv.at[h, r, step - 1],
            device(y, z, c, to),
        )
        copy.start()
        results.append((h, r, copy))

    for step in (2, 1, 3, 0):
        pick(0, step, (0, 1, 2))
    arrived(down_2[0])
    for copy in hid_far[0] + hid_far[1]:
        copy.wait_recv()
    for step in (2, 1, 3, 0):
        pick(0, step, (3,))
        project(0, 0, step)
    arrived(down_2[1])
    for step in (2, 1, 3, 0):
        project(0, 1, step)
    for step in (2, 1, 3, 0):
        pick(1, step, (0, 1, 2, 3))
        project(1, 0, step)
        project(1, 1, step)
    arrived(down_2[2])
    for h in (0, 1):
        for step in (2, 1, 3, 0):
            project(h, 2, step)

    load_order.wait()

    def ordered(h, half, matrix, last):
        table = inbox[matrix].reshape(RING * OUTB, OUTB)

        def pieces(n, r):
            left = table[n * OUTB : (n + 1) * OUTB, r * LANES : (r + 1) * LANES]
            return left, fin[n, h, r, :, half * LANES : (half + 1) * LANES]

        result = None
        for n in range(0, RING, 2):
            for pair in [[(n, 2), (n + 1, 2)]] if last else [[(n, 0), (n, 1)], [(n + 1, 0), (n + 1, 1)]]:
                left, right = zip(*[pieces(*at) for at in pair])
                part = lax.dot_general(
                    jnp.concatenate(left, axis=1),
                    jnp.concatenate(right, axis=1),
                    (((1,), (1,)), ((), ())),
                    preferred_element_type=F32,
                )
                result = part if result is None else result + part
        return result

    def keep(b, h):
        rows = pl.ds(pl.multiple_of(b * OUTB, OUTB), OUTB) if not isinstance(b, int) else pl.ds(b * OUTB, min(OUTB, D - b * OUTB))
        spot = (rows, slice(h * BLOCK, (h + 1) * BLOCK))
        return spot, pltpu.make_async_copy(made_out.at[spot], out.at[spot], made_sem.at[h, b])

    def store(b, h, value, last):
        spot, copy = keep(b, h)
        if last:
            made_out[spot] = (made_out[spot].astype(F32) + value).astype(BF16)
            copy.start()
        else:
            made_out[spot] = value.astype(BF16)

    outgoing = {last: [copy for _, r, copy in results if (r == 2) == last] for last in (False, True)}

    def settle():
        sent(1)
        for cc in (0, 1):
            for h in (0, 1):
                own, _, far = shuffle(cc, h, everything)
                pl.when(jnp.logical_not(own))(far.wait_send)
        for copies in (second_0, second_1, *down_1, *down_2):
            for copy in copies[1]:
                copy.wait_send()
        for copy in tok_near + tok_far + sum(hid_near + hid_far, []) + outgoing[False]:
            copy.wait_send()

    for last in (False, True):
        if last:
            settle()
        for h in (0, 1):
            for hh, r, copy in results:
                if hh == h and (r == 2) == last:
                    copy.wait_recv()

            @pl.loop(0, 3, unroll=3)
            def _(b):
                store(b, h, ordered(h, 0, b, last), last)

            store(3, h, ordered(h, 0, 3, last) + ordered(h, 1, 8, last), last)

            @pl.loop(4, 7, unroll=3)
            def _(b):
                store(b, h, ordered(h, 1, b, last), last)

            store(7, h, ordered(h, 1, 7, last)[: D - 7 * OUTB], last)

    for copy in outgoing[True]:
        copy.wait_send()
    for h in (0, 1):
        for b in range(8):
            keep(b, h)[1].wait()


def body(tokens, gate_weight, up_weight, down_weight, block_counts, block_tokens):
    vmem, hbm = pl.BlockSpec(memory_space=pltpu.VMEM), pl.BlockSpec(memory_space=pltpu.HBM)
    dma = pltpu.SemaphoreType.DMA
    made = pl.pallas_call(
        kernel,
        out_shape=(
            jax.ShapeDtypeStruct((D, 2 * BLOCK), BF16),
            jax.ShapeDtypeStruct((2, 2, RING, RING, 2, PAD, COLS), BF16),
            jax.ShapeDtypeStruct((RING, 2, RING, RING, 48, COLS), BF16),
            jax.ShapeDtypeStruct((2, CHUNKS, RING, RING, RING, TILE, COLS), BF16),
            jax.ShapeDtypeStruct((RING, FEAT, TOK), BF16),
        ),
        in_specs=[hbm, hbm, hbm, hbm, vmem, pl.BlockSpec(memory_space=pltpu.SMEM), vmem, vmem, vmem, hbm],
        out_specs=(hbm, hbm, hbm, hbm, hbm),
        scratch_shapes=[
            pltpu.VMEM((2, 2, RING, RING, 2, PAD, COLS), BF16),
            pltpu.VMEM((9, RING, 2, 2, PAD, COLS), BF16),
            pltpu.VMEM((RING, TOK, WIDE), BF16),
            pltpu.VMEM((2, 2, PAD, 16, COLS), BF16),
            *[pltpu.VMEM((2, RING, RING, RING, TILE, COLS), BF16) for _ in range(CHUNKS)],
            *[pltpu.VMEM((2, TOK, COLS), BF16) for _ in range(RING)],
            pltpu.VMEM((3, 2, CHUNKS, BLOCK, BLOCK), BF16),
            pltpu.VMEM((RING, 2, CHUNKS, BLOCK, BLOCK), BF16),
            pltpu.VMEM((SLOTS, BLOCK, LANES), jnp.int32),
            pltpu.VMEM((2, FEAT, TOK), BF16),
            pltpu.VMEM((D, 2 * BLOCK), BF16),
            dma((2, 2)),
            dma,
            dma((2,)),
            dma((2, 8)),
            dma((2, 2, RING)), dma((2, 2, RING)),
            dma((2, 2, RING, 2)), dma((2, 2, RING, 2)),
            dma((2, 2)), dma((RING,)),
            dma((2, CHUNKS, RING)), dma((2, CHUNKS, RING)),
            dma((2, CHUNKS, RING)), dma((2, CHUNKS, RING)),
            dma((RING,)), dma((RING,)),
            dma((2, RING)), dma((2, RING)),
            dma((2, CHUNKS, 3)), dma((2, CHUNKS, 3)),
        ],
        compiler_params=pltpu.CompilerParams(
            collective_id=0, has_side_effects=True, vmem_limit_bytes=60 * 2**20
        ),
    )(
        tokens.T,
        *[jnp.swapaxes(weight, 0, 1) for weight in (gate_weight, up_weight, down_weight)],
        block_tokens,
        block_counts,
        jnp.asarray(place_matrix(), BF16),
        jnp.asarray(group_matrix(), BF16),
        jnp.asarray(swap_matrix(), BF16),
        jnp.asarray(order_matrix(), BF16).reshape(9, RING, 2, 2, PAD, COLS),
    )
    return made[0].T


def solution(mesh):
    in_specs = (
        P("expert", "shard"),
        P(None, "expert", "shard"),
        P(None, "expert", "shard"),
        P(None, "expert", "shard"),
        P("expert"),
        P("expert", None),
    )
    out_specs = P(("expert", "shard"), None)
    return jax.shard_map(body, mesh=mesh, in_specs=in_specs, out_specs=out_specs, check_vma=False)
```
